32 devices in a mesh: grp: 2 (over y), tm: 4 (over z), sub: 2 (over x), ch: 2 (over core).
Axes of the slice: x: 2, y: 2, z: 4, core: 2. Of those that a mesh axis runs over, the one named last changes fastest.
Arguments:
- archive: float32 [16, 16384], P('ch', ('grp', 'tm')), parts along dimension 1, may hold values from -6 to 6
- tail: float32 [16, 254], P(None, 'grp'), parts along dimension 1, may hold values from -6 to 6
- precision: float32 [16, 16], replicated, may hold values from -1.5 to 1.5
- tile_list: int32 [8, 2, 2, 2], P(('grp', 'tm'), 'sub'), parts along dimension 0, may hold values from 0 to 15, as said below
Outputs:
- profile: float32 [16384], P(('grp', 'tm', 'sub')), parts along dimension 0
The draws below stay inside these ranges and needn't reach their ends.
There are 2 independent parts, one for each index of `grp`. The reference program is written for one: setup_inputs(seed, part) draws one part's arguments, and reference() takes and returns one part's arrays. A program takes and returns all parts, laid end to end along the dimension named above; an argument that names none is the same for every part. Nothing has to cross between parts.
Inputs may be any that keep to these rules, and one draw needn't show every extreme that they name: `tile_list`: each pair has row block <= column block; every block k < 16 appears in some pair; pairs may repeat.
All inputs are finite; a program needn't handle non-finite values.
Results may differ from the reference program's by a relative error of at most 0.0003.
Values may be sent and summed in bfloat16 or wider, within the bound.
A program may use at most 128 MiB of HBM per device.

```python
import jax
import jax.numpy as jnp
from jax import lax

C = 16
M = 128
TS = 512
SLOTS = 2
DEPTH = 2048
EXCL = 32
NB = 16
NS = 8192
N_TM = 4
N_SUB = 2


def draw_tile_list(key, part):
    slot_count = N_TM * N_SUB * SLOTS
    order_blocks = jax.random.permutation(jax.random.fold_in(key, 11), NB).astype(jnp.int32)
    if NB % 2 == 1:
        order_blocks = jnp.concatenate([order_blocks, order_blocks[-1:]])
    first = order_blocks[0::2]
    second = order_blocks[1::2]
    covering = first.shape[0]
    extra_first = jax.random.randint(jax.random.fold_in(key, 13), (slot_count - covering,), 0, NB).astype(jnp.int32)
    extra_second = jax.random.randint(jax.random.fold_in(key, 17), (slot_count - covering,), 0, NB).astype(jnp.int32)
    left = jnp.concatenate([first, extra_first])
    right = jnp.concatenate([second, extra_second])
    lower = jnp.minimum(left, right)
    upper = jnp.maximum(left, right)
    shuffle = jax.random.permutation(jax.random.fold_in(key, 23), slot_count)
    pairs_out = jnp.stack([lower[shuffle], upper[shuffle]], axis=-1)
    return pairs_out.reshape(N_TM, N_SUB, SLOTS, 2).astype(jnp.int32)


def levels(rng, extent, shards, low, largest):
    def one(position, shards_of):
        steps = jax.random.uniform(jax.random.fold_in(jax.random.fold_in(rng, 6), position), (shards_of,), jnp.float32, low / len(shards), largest / len(shards))
        return jnp.repeat(jnp.exp(steps), extent[position] // shards_of).reshape((-1,) + (1,) * (len(extent) - position - 1))

    loudness = one(*shards[0])
    for cut in shards[1:]:
        loudness = loudness * one(*cut)
    return loudness


def normal_values(key, dims, spread, bound, shards=(), kind=jnp.bfloat16):
    values = spread * jax.random.normal(key, dims, jnp.float32)
    if shards:
        values = values * levels(key, dims, shards, -0.22, 0.18)
    return jnp.clip(values, -bound, bound).astype(kind)


def setup_inputs(seed: int = 0, part: int = 0) -> dict:
    streams_of = jax.random.split(jax.random.key(seed), 5)
    own_keys = jax.random.split(jax.random.fold_in(streams_of[4], part), 5)
    return {
        "archive": normal_values(own_keys[0], (C, NS), 1.0, 6.0, ((0, 2), (1, 4)), jnp.float32),
        "tail": normal_values(own_keys[1], (C, M - 1), 1.0, 6.0, (), jnp.float32),
        "precision": normal_values(streams_of[2], (C, C), C ** -0.5, 1.5, (), jnp.float32),
        "tile_list": draw_tile_list(jax.random.fold_in(jax.random.fold_in(streams_of[4], part), 71), part),
    }


def whiten(factor, samples):
    return jnp.dot(factor, samples, precision=lax.Precision.HIGHEST, preferred_element_type=jnp.float32).astype(jnp.bfloat16)


def build_rows(series_wide, start):
    segment = lax.dynamic_slice_in_dim(series_wide, start, TS + M - 1, 1)
    return jnp.stack([segment[:, offset:offset + TS] for offset in range(M)]).reshape(M * C, TS)


def lower_into(profile, values, start):
    current = lax.dynamic_slice_in_dim(profile, start, values.shape[0])
    return lax.dynamic_update_slice_in_dim(profile, jnp.minimum(current, values), start, 0)


def reference(archive, tail, precision, tile_list):
    series = jnp.concatenate([whiten(precision, archive), whiten(precision, tail)], axis=1)
    series_wide = series.astype(jnp.float32)
    squares = jnp.sum(series_wide * series_wide, axis=0)
    window_norms = lax.reduce_window(squares, jnp.array(0, squares.dtype), lax.add, (M,), (1,), "VALID")
    tile_pairs = tile_list.reshape(-1, 2).astype(jnp.int32)

    def one_pair(profile, pair):
        row_start = (pair[0] * TS).astype(jnp.int32)
        col_start = (pair[1] * TS).astype(jnp.int32)
        row_hankel = build_rows(series_wide, row_start)
        col_hankel = build_rows(series_wide, col_start)
        products = jnp.dot(row_hankel.T, col_hankel, precision=lax.Precision.HIGHEST)
        row_norms = lax.dynamic_slice_in_dim(window_norms, row_start, TS)
        col_norms = lax.dynamic_slice_in_dim(window_norms, col_start, TS)
        distance = (row_norms[:, None] + col_norms[None, :] - 2.0 * products) / DEPTH
        row_index = row_start + jnp.arange(TS).astype(jnp.int32)
        col_index = col_start + jnp.arange(TS).astype(jnp.int32)
        too_near = jnp.abs(row_index[:, None] - col_index[None, :]) < EXCL
        distance = jnp.where(too_near, jnp.inf, distance)
        profile = lower_into(profile, jnp.min(distance, axis=1), row_start)
        profile = lower_into(profile, jnp.min(distance, axis=0), col_start)
        return profile, None

    start_profile = jnp.full((NS,), jnp.inf, jnp.float32)
    profile, unused = lax.scan(one_pair, start_profile, tile_pairs)
    return profile
```

```python
import functools

import jax
import jax.numpy as jnp
from jax import lax
from jax.experimental import pallas as pl
from jax.experimental.pallas import tpu as pltpu
from jax.sharding import PartitionSpec as P

M = 128
TS = 512
SLOTS = 2
DEPTH = 2048
EXCL = 32
LANES = 128
STEP = 16
MESH = pl.DeviceIdType.MESH


def whiten(factor, samples):
    return jnp.dot(
        factor, samples, precision=lax.Precision.HIGHEST, preferred_element_type=jnp.float32
    ).astype(jnp.bfloat16)


def gather_kernel(
    n_tm,
    n_sub,
    tiles_hbm,
    archive_hbm,
    tail_hbm,
    precision_hbm,
    series_ref,
    lists_ref,
    tail_ref,
    precision_ref,
    raw_ref,
    load_sems,
    raw_sems,
    time_send,
    time_recv,
    pair_send,
    pair_recv,
    list_send,
    list_recv,
    lists_send,
    lists_recv,
    time_here,
    sub_here,
):
    tm, sub, ch = lax.axis_index("tm"), lax.axis_index("sub"), lax.axis_index("ch")
    other = 1 - ch
    channels, span = archive_hbm.shape
    half = span // 2
    tiles = half // LANES
    last = n_tm * span // LANES

    def send(source, target, sem, landed, device):
        return pltpu.make_async_remote_copy(
            src_ref=source,
            dst_ref=target,
            send_sem=sem,
            recv_sem=landed,
            device_id=device,
            device_id_type=MESH,
        )

    def others(axis, size, here):
        for step in range(size - 1):
            yield step, step >= here, {axis: step + (step + size - here) // size}

    barrier = pltpu.get_barrier_semaphore()
    pl.semaphore_signal(barrier, inc=1, device_id={"ch": other}, device_id_type=MESH)
    for axis, size, here in (("tm", n_tm, tm), ("sub", n_sub, sub)):
        for step, after, device in others(axis, size, here):

            @pl.when(after)
            def _():
                pl.semaphore_signal(barrier, inc=1, device_id=device, device_id_type=MESH)

    own_rows = pl.ds(pl.multiple_of(ch * channels, channels), channels)
    own_half = archive_hbm.at[:, pl.ds(pl.multiple_of(ch * half, half), half)]
    own_list = lists_ref.at[sub, tm]
    loads = [
        pltpu.make_async_copy(source, target, load_sems.at[at])
        for at, (source, target) in enumerate(
            (
                (precision_hbm, precision_ref),
                (tail_hbm, tail_ref),
                (own_half, raw_ref.at[own_rows, :]),
                (tiles_hbm.at[0, 0], own_list),
            )
        )
    ]
    for load in loads:
        load.start()
    pl.semaphore_wait(barrier, 1 + tm + sub)

    swap = send(
        archive_hbm.at[:, pl.ds(pl.multiple_of(other * half, half), half)],
        raw_ref.at[own_rows, :],
        raw_sems.at[0],
        raw_sems.at[1],
        {"ch": other},
    )
    swap.start()
    for axis, size, here, semaphores in (("tm", n_tm, tm, time_here), ("sub", n_sub, sub, sub_here)):
        for step, after, device in others(axis, size, here):

            @pl.when(jnp.logical_not(after))
            def _():
                pl.semaphore_signal(
                    semaphores.at[here], inc=1, device_id=device, device_id_type=MESH
                )

    list_along = [
        send(tiles_hbm.at[0, 0], own_list, list_send.at[step], list_recv.at[tm], device)
        for step, _, device in others("tm", n_tm, tm)
    ]
    for step, after, _ in others("tm", n_tm, tm):
        pl.when(jnp.logical_not(after))(list_along[step].start)
    for load in loads[:2]:
        load.wait()
    factor = precision_ref[...]
    series_ref[last] = jnp.zeros((2 * channels, LANES), jnp.bfloat16)
    series_ref[last, :, : M - 1] = whiten(factor, tail_ref[...])
    for load in loads[2:]:
        load.wait()
    swap.wait_recv()

    def chunk(owner, part):
        return series_ref.at[pl.ds((owner * 2 + part) * tiles, tiles)]

    mine = chunk(tm, ch)
    whitened = whiten(factor, raw_ref[...])
    for k in range(tiles):
        series_ref[(tm * 2 + ch) * tiles + k] = whitened[:, k * LANES : (k + 1) * LANES]
    along_time = [
        send(mine, mine, time_send.at[step], time_recv.at[tm], device)
        for step, _, device in others("tm", n_tm, tm)
    ]
    to_pair = []

    def forward(held):
        step = len(to_pair)
        copy = send(held, held, pair_send.at[step], pair_recv.at[step], {"ch": other})
        to_pair.append(copy)
        copy.start()

    for step, after, device in others("tm", n_tm, tm):

        @pl.when(after)
        def _():
            pl.semaphore_wait(time_here.at[device["tm"]], 1)
            list_along[step].start()

        along_time[step].start()
    forward(mine)
    lists_along = []
    for step in range(1, n_tm):
        if step == n_tm - 1:
            for back in range(1, n_tm):
                source = back + ((tm + n_tm - back) // n_tm) * (tm - 2 * back)
                held = lists_ref.at[sub, source]
                send(held, held, list_send.at[0], list_recv.at[source], {"ch": other}).wait_recv()
            held = lists_ref.at[sub]
            for at, after, device in others("sub", n_sub, sub):
                pl.when(after)(
                    functools.partial(pl.semaphore_wait, sub_here.at[device["sub"]], 1)
                )
                copy = send(held, held, lists_send.at[at], lists_recv.at[sub], device)
                lists_along.append(copy)
                copy.start()
        source = step + ((tm + n_tm - step) // n_tm) * (tm - 2 * step)
        held = chunk(source, ch)
        send(held, held, time_send.at[0], time_recv.at[source], {"ch": other}).wait_recv()
        forward(held)
    for at, _, device in others("sub", n_sub, sub):
        held = lists_ref.at[device["sub"]]
        send(held, held, lists_send.at[0], lists_recv.at[device["sub"]], {"ch": other}).wait_recv()
    for copy in to_pair:
        copy.wait_recv()
    for copy in [swap] + list_along + along_time + lists_along + to_pair:
        copy.wait_send()


def match_kernel(
    n_sub,
    series_ref,
    lists_ref,
    out_ref,
    lists_smem,
    work_smem,
    hankel_ref,
    lagged_ref,
    mine_ref,
    wide_ref,
    near_ref,
    products_ref,
    best_ref,
    list_sem,
):
    copy = pltpu.make_async_copy(lists_ref, lists_smem, list_sem)
    copy.start()
    units, unit_cols, depth = mine_ref.shape
    channels = depth // STEP
    n_tiles = unit_cols // LANES
    unit = unit_cols - M
    per_block = TS // LANES
    rows = TS + M
    ch = lax.axis_index("ch")
    me = lax.axis_index("tm") * n_sub + lax.axis_index("sub")
    own_tile = me * (units * unit // LANES)
    identity = (
        lax.broadcasted_iota(jnp.int32, (depth, depth), 0)
        == lax.broadcasted_iota(jnp.int32, (depth, depth), 1)
    )

    def lag(first_tile, count, scale):
        segment = jnp.concatenate([series_ref[first_tile + k] for k in range(count)], axis=1)
        segment = segment.astype(jnp.float32)
        width = count * LANES
        for l in range(STEP):
            moved = segment if l == 0 else pltpu.roll(segment, width - l, axis=1)
            hankel_ref[l * channels : (l + 1) * channels, :width] = moved.astype(jnp.bfloat16)
        scaled = jnp.where(identity, scale, 0.0).astype(jnp.bfloat16)
        lagged = []
        for at in range(0, width, depth):
            size = min(depth, width - at)
            lagged.append(
                lax.dot_general(
                    scaled[:size, :size] if size == depth else jnp.where(
                        lax.broadcasted_iota(jnp.int32, (size, size), 0)
                        == lax.broadcasted_iota(jnp.int32, (size, size), 1), scale, 0.0
                    ).astype(jnp.bfloat16),
                    hankel_ref[:, at : at + size],
                    (((1,), (1,)), ((), ())),
                    preferred_element_type=jnp.float32,
                ).astype(jnp.bfloat16)
            )
        norms = jnp.broadcast_to(jnp.sum(segment * segment, axis=0, keepdims=True), (8, width))
        shift = 1
        while shift < M:
            norms = norms + pltpu.roll(norms, width - shift, axis=1)
            shift *= 2
        return lagged, norms

    lagged, own_norms = lag(own_tile, units * unit // LANES + 1, 1.0)
    groups = [
        piece[at : at + STEP] for piece in lagged for at in range(0, piece.shape[0], STEP)
    ]
    for u in range(units):
        for q in range(unit_cols // STEP):
            place = ((q % n_tiles) * 8 + q // n_tiles) * STEP
            mine_ref[u, place : place + STEP, :] = groups[u * unit // STEP + q]
        best_ref[u] = jnp.full((8, unit_cols), jnp.inf, jnp.float32)
    lane = lax.broadcasted_iota(jnp.int32, (8, LANES), 1)
    own_at = [((lane // STEP) * n_tiles + t) * STEP + lane % STEP for t in range(n_tiles)]
    sublane = lax.broadcasted_iota(jnp.int32, (8, LANES), 0)

    copy.wait()
    owners, n_tm = lists_smem.shape[0] * lists_smem.shape[1], lists_smem.shape[1]

    def scan(owner, found):
        for slot in range(SLOTS):
            listed = (owner // n_tm, owner % n_tm, slot)
            row_block, col_block = lists_smem[(*listed, 0)], lists_smem[(*listed, 1)]
            for u in range(units):
                block = (own_tile * LANES + u * unit) // TS
                work_smem[found] = (row_block + col_block - block) * units + u
                hit = (row_block == block) | (col_block == block)
                found = found + hit.astype(jnp.int32)
        return found

    if owners <= 16:
        found = jnp.int32(0)
        for owner in range(owners):
            found = scan(owner, found)
    else:
        found = lax.fori_loop(0, owners, scan, jnp.int32(0))

    def ahead(tiles, at):
        turn = at // n_tiles
        tile = tiles[at % n_tiles]
        return tile if turn == 0 else pltpu.roll(tile, LANES - turn * STEP, axis=1)

    def keep_apart(offset):
        for g in range(0, (TS + M) // STEP, M // STEP):
            for at in range(g * STEP, (g + 1) * STEP, 8):
                for t in range(n_tiles):
                    here = (pl.ds(at, 8), pl.ds(t * LANES, LANES))
                    apart = (sublane + (at + offset)) - own_at[t]
                    products_ref[here] = jnp.where(
                        jnp.abs(apart) < EXCL, jnp.inf, products_ref[here]
                    )

    def reduce(u):
        run = TS // STEP

        def some(turn, low):
            part = turn % (STEP // 8)
            first = (turn // (STEP // 8)) * (run * STEP) + part * 8
            ones, twos, fours = {}, {}, {}
            low = list(low)
            for g in range(run + 7):
                ones[g] = [
                    products_ref[pl.ds(first + g * STEP, 8), t * LANES : (t + 1) * LANES]
                    for t in range(n_tiles)
                ]
                if g >= 1:
                    twos[g - 1] = [
                        ones[g - 1][t] + ahead(ones[g], t + 1) for t in range(n_tiles)
                    ]
                if g >= 3:
                    fours[g - 3] = [
                        twos[g - 3][t] + ahead(twos[g - 1], t + 2) for t in range(n_tiles)
                    ]
                if g >= 7:
                    wide = wide_ref[pl.ds(first + (g - 7) * STEP, 8), :]
                    for t in range(n_tiles):
                        score = fours[g - 7][t] + ahead(fours[g - 3], t + 4) + wide
                        low[t] = jnp.minimum(low[t], score)
            return tuple(low)

        low = tuple(best_ref[u, :, t * LANES : (t + 1) * LANES] for t in range(n_tiles))
        for turn in range(TS // run // STEP * (STEP // 8)):
            low = some(turn, low)
        for t in range(n_tiles):
            best_ref[u, :, t * LANES : (t + 1) * LANES] = low[t]

    def incidence(at, _):
        entry = work_smem[2 * at + ch]
        u = entry % units
        partner = entry // units
        lagged, norms = lag(partner * per_block, rows // LANES, -2.0)
        place = 0
        for piece in lagged:
            lagged_ref[place : place + piece.shape[0], :] = piece
            place += piece.shape[0]
        for k in range(per_block):
            one = jnp.broadcast_to(norms[:1, k * LANES : (k + 1) * LANES], (LANES, LANES))
            wide_ref[k * LANES : (k + 1) * LANES, :] = jnp.transpose(one)
        products_ref[...] = lax.dot_general(
            lagged_ref[...], mine_ref[u], (((1,), (1,)), ((), ())), preferred_element_type=jnp.float32
        )
        offset = partner * TS - (own_tile * LANES + u * unit)
        keep_apart(offset)
        reduce(u)
        return 0

    lax.fori_loop(0, (found + 1 - ch) // 2, incidence, 0)

    group = lane // STEP
    for u in range(units):
        low = jnp.min(best_ref[u], axis=0, keepdims=True)
        tiles = [
            jnp.broadcast_to(low[:, t * LANES : (t + 1) * LANES], (8, LANES)) for t in range(n_tiles)
        ]
        for k in range(unit // LANES):
            natural = None
            for g in range(LANES // STEP):
                q = k * (LANES // STEP) + g
                turn = (g - q // n_tiles) % (LANES // STEP)
                tile = tiles[q % n_tiles]
                tile = tile if turn == 0 else pltpu.roll(tile, turn * STEP, axis=1)
                natural = tile if natural is None else jnp.where(group == g, tile, natural)
            at = u * (unit // LANES) + k
            done = (natural[:1] + own_norms[:1, at * LANES : (at + 1) * LANES]) * (1.0 / DEPTH)
            out_ref[at : at + 1, :] = done


def swap_kernel(mine_ref, theirs_ref, sems):
    other = {"ch": 1 - lax.axis_index("ch")}
    barrier = pltpu.get_barrier_semaphore()
    pl.semaphore_signal(barrier, inc=1, device_id=other, device_id_type=MESH)
    pl.semaphore_wait(barrier, 1)
    copy = pltpu.make_async_remote_copy(
        src_ref=mine_ref,
        dst_ref=theirs_ref,
        send_sem=sems.at[0],
        recv_sem=sems.at[1],
        device_id=other,
        device_id_type=MESH,
    )
    copy.start()
    copy.wait()


def lower_kernel(mine_ref, theirs_ref, out_ref):
    out_ref[...] = jnp.minimum(mine_ref[...], theirs_ref[...])


def body(archive, tail, precision, tile_list):
    n_tm, n_sub = lax.axis_size("tm"), lax.axis_size("sub")
    owners = n_tm * n_sub
    channels, span = archive.shape
    piece = span // n_sub
    unit = min(piece, TS)
    units = piece // unit
    every = 2 * channels
    depth = STEP * every
    most = max(piece, TS) + M
    anywhere = pl.BlockSpec(memory_space=pltpu.HBM)
    inside = pl.BlockSpec(memory_space=pltpu.VMEM)
    series, lists = pl.pallas_call(
        functools.partial(gather_kernel, n_tm, n_sub),
        out_shape=[
            pltpu.VMEM((n_tm * span // LANES + 1, every, LANES), jnp.bfloat16),
            pltpu.VMEM((n_sub, n_tm) + tile_list.shape[2:], jnp.int32),
        ],
        in_specs=[anywhere] * 4,
        out_specs=[inside] * 2,
        scratch_shapes=[
            pltpu.VMEM(tail.shape, jnp.float32),
            pltpu.VMEM(precision.shape, jnp.float32),
            pltpu.VMEM((every, span // 2), jnp.float32),
            pltpu.SemaphoreType.DMA((4,)),
            pltpu.SemaphoreType.DMA((2,)),
            pltpu.SemaphoreType.DMA((n_tm,)),
            pltpu.SemaphoreType.DMA((n_tm,)),
            pltpu.SemaphoreType.DMA((n_tm,)),
            pltpu.SemaphoreType.DMA((n_tm,)),
            pltpu.SemaphoreType.DMA((n_tm,)),
            pltpu.SemaphoreType.DMA((n_tm,)),
            pltpu.SemaphoreType.DMA((n_sub,)),
            pltpu.SemaphoreType.DMA((n_sub,)),
            pltpu.SemaphoreType.REGULAR((n_tm,)),
            pltpu.SemaphoreType.REGULAR((n_sub,)),
        ],
        compiler_params=pltpu.CompilerParams(
            collective_id=0, has_side_effects=True, vmem_limit_bytes=62 * 2**20
        ),
    )(tile_list, archive, tail, precision)
    series = pltpu.with_memory_space_constraint(series, pltpu.VMEM)
    lists = pltpu.with_memory_space_constraint(lists, pltpu.VMEM)
    shape = (piece // LANES, LANES)
    mine = pl.pallas_call(
        functools.partial(match_kernel, n_sub),
        out_shape=pltpu.VMEM(shape, jnp.float32),
        in_specs=[inside] * 2,
        out_specs=inside,
        scratch_shapes=[
            pltpu.SMEM(lists.shape, jnp.int32),
            pltpu.SMEM((owners * SLOTS * units + 1,), jnp.int32),
            pltpu.VMEM((depth, most), jnp.bfloat16),
            pltpu.VMEM((TS + M, depth), jnp.bfloat16),
            pltpu.VMEM((units, unit + M, depth), jnp.bfloat16),
            pltpu.VMEM((TS, LANES), jnp.float32),
            pltpu.VMEM((8, LANES), jnp.float32),
            pltpu.VMEM((TS + M, unit + M), jnp.float32),
            pltpu.VMEM((units, 8, unit + M), jnp.float32),
            pltpu.SemaphoreType.DMA,
        ],
        compiler_params=pltpu.CompilerParams(vmem_limit_bytes=32 * 2**20),
    )(series, lists)
    mine = pltpu.with_memory_space_constraint(mine, pltpu.VMEM)
    theirs = pl.pallas_call(
        swap_kernel,
        out_shape=pltpu.VMEM(shape, jnp.float32),
        in_specs=[inside],
        out_specs=inside,
        scratch_shapes=[pltpu.SemaphoreType.DMA((2,))],
        compiler_params=pltpu.CompilerParams(
            collective_id=1, has_side_effects=True, vmem_limit_bytes=16 * 2**20
        ),
    )(mine)
    theirs = pltpu.with_memory_space_constraint(theirs, pltpu.VMEM)
    out = pl.pallas_call(
        lower_kernel,
        out_shape=jax.ShapeDtypeStruct(shape, jnp.float32),
        in_specs=[inside] * 2,
        out_specs=inside,
        compiler_params=pltpu.CompilerParams(vmem_limit_bytes=16 * 2**20),
    )(mine, theirs)
    return out.reshape(-1)


def solution(mesh):
    placed = (P("ch", ("grp", "tm")), P(None, "grp"), P(), P(("grp", "tm"), "sub", None, None))
    return jax.shard_map(
        body, mesh=mesh, in_specs=placed, out_specs=P(("grp", "tm", "sub")), check_vma=False
    )
```

```python
import functools

import jax
import jax.numpy as jnp
from jax import lax
from jax.experimental import pallas as pl
from jax.experimental.pallas import tpu as pltpu
from jax.sharding import PartitionSpec as P

M = 128
TS = 512
SLOTS = 2
DEPTH = 2048
EXCL = 32
LANES = 128
STEP = 16
MESH = pl.DeviceIdType.MESH


def whiten(factor, samples):
    return jnp.dot(
        factor, samples, precision=lax.Precision.HIGHEST, preferred_element_type=jnp.float32
    ).astype(jnp.bfloat16)


def gather_kernel(
    n_tm,
    n_sub,
    tiles_hbm,
    archive_hbm,
    tail_hbm,
    precision_hbm,
    series_ref,
    lists_ref,
    tail_ref,
    precision_ref,
    raw_ref,
    load_sems,
    raw_sems,
    time_send,
    time_recv,
    pair_send,
    pair_recv,
    list_send,
    list_recv,
    lists_send,
    lists_recv,
    time_here,
    sub_here,
):
    tm, sub, ch = lax.axis_index("tm"), lax.axis_index("sub"), lax.axis_index("ch")
    other = 1 - ch
    channels, span = archive_hbm.shape
    half = span // 2
    tiles = half // LANES
    last = n_tm * span // LANES

    def send(source, target, sem, landed, device):
        return pltpu.make_async_remote_copy(
            src_ref=source,
            dst_ref=target,
            send_sem=sem,
            recv_sem=landed,
            device_id=device,
            device_id_type=MESH,
        )

    def others(axis, size, here):
        for step in range(size - 1):
            yield step, step >= here, {axis: step + (step + size - here) // size}

    barrier = pltpu.get_barrier_semaphore()
    pl.semaphore_signal(barrier, inc=1, device_id={"ch": other}, device_id_type=MESH)
    for axis, size, here in (("tm", n_tm, tm), ("sub", n_sub, sub)):
        for step, after, device in others(axis, size, here):

            @pl.when(after)
            def _():
                pl.semaphore_signal(barrier, inc=1, device_id=device, device_id_type=MESH)

    own_rows = pl.ds(pl.multiple_of(ch * channels, channels), channels)
    own_half = archive_hbm.at[:, pl.ds(pl.multiple_of(ch * half, half), half)]
    own_list = lists_ref.at[tm, sub]
    loads = [
        pltpu.make_async_copy(source, target, load_sems.at[at])
        for at, (source, target) in enumerate(
            (
                (precision_hbm, precision_ref),
                (tail_hbm, tail_ref),
                (own_half, raw_ref.at[own_rows, :]),
                (tiles_hbm.at[0, 0], own_list),
            )
        )
    ]
    for load in loads:
        load.start()
    pl.semaphore_wait(barrier, 1 + tm + sub)

    swap = send(
        archive_hbm.at[:, pl.ds(pl.multiple_of(other * half, half), half)],
        raw_ref.at[own_rows, :],
        raw_sems.at[0],
        raw_sems.at[1],
        {"ch": other},
    )
    swap.start()
    for axis, size, here, semaphores in (("tm", n_tm, tm, time_here), ("sub", n_sub, sub, sub_here)):
        for step, after, device in others(axis, size, here):

            @pl.when(jnp.logical_not(after))
            def _():
                pl.semaphore_signal(
                    semaphores.at[here], inc=1, device_id=device, device_id_type=MESH
                )

    lists_along = [
        send(tiles_hbm.at[0, 0], own_list, lists_send.at[step], lists_recv.at[sub], device)
        for step, _, device in others("sub", n_sub, sub)
    ]
    for step, after, _ in others("sub", n_sub, sub):
        pl.when(jnp.logical_not(after))(lists_along[step].start)
    for load in loads[:2]:
        load.wait()
    factor = precision_ref[...]
    series_ref[last] = jnp.zeros((2 * channels, LANES), jnp.bfloat16)
    series_ref[last, :, : M - 1] = whiten(factor, tail_ref[...])
    for load in loads[2:]:
        load.wait()
    swap.wait_recv()

    def chunk(owner, part):
        return series_ref.at[pl.ds((owner * 2 + part) * tiles, tiles)]

    mine = chunk(tm, ch)
    whitened = whiten(factor, raw_ref[...])
    for k in range(tiles):
        series_ref[(tm * 2 + ch) * tiles + k] = whitened[:, k * LANES : (k + 1) * LANES]
    along_time = [
        send(mine, mine, time_send.at[step], time_recv.at[tm], device)
        for step, _, device in others("tm", n_tm, tm)
    ]
    to_pair = []

    def forward(held):
        step = len(to_pair)
        copy = send(held, held, pair_send.at[step], pair_recv.at[step], {"ch": other})
        to_pair.append(copy)
        copy.start()

    for step, after, _ in others("tm", n_tm, tm):
        pl.when(jnp.logical_not(after))(along_time[step].start)
    forward(mine)
    for step, after, device in others("sub", n_sub, sub):

        @pl.when(after)
        def _():
            pl.semaphore_wait(sub_here.at[device["sub"]], 1)
            lists_along[step].start()

    for step, after, device in others("tm", n_tm, tm):

        @pl.when(after)
        def _():
            pl.semaphore_wait(time_here.at[device["tm"]], 1)
            along_time[step].start()

    for _, _, device in others("sub", n_sub, sub):
        held = lists_ref.at[tm, device["sub"]]
        send(held, held, lists_send.at[0], lists_recv.at[device["sub"]], {"ch": other}).wait_recv()
    held = lists_ref.at[tm]
    list_along = [
        send(held, held, list_send.at[step], list_recv.at[tm], device)
        for step, _, device in others("tm", n_tm, tm)
    ]
    for copy in list_along:
        copy.start()
    for step in range(1, n_tm):
        source = step + ((tm + n_tm - step) // n_tm) * (tm - 2 * step)
        held = chunk(source, ch)
        send(held, held, time_send.at[0], time_recv.at[source], {"ch": other}).wait_recv()
        forward(held)
    for _, _, device in others("tm", n_tm, tm):
        held = lists_ref.at[device["tm"]]
        send(held, held, list_send.at[0], list_recv.at[device["tm"]], {"ch": other}).wait_recv()
    for copy in to_pair:
        copy.wait_recv()
    for copy in [swap] + list_along + along_time + lists_along + to_pair:
        copy.wait_send()


def match_kernel(
    n_sub,
    series_ref,
    lists_ref,
    out_ref,
    lists_smem,
    work_smem,
    hankel_ref,
    lagged_ref,
    mine_ref,
    wide_ref,
    near_ref,
    products_ref,
    best_ref,
    list_sem,
):
    copy = pltpu.make_async_copy(lists_ref, lists_smem, list_sem)
    copy.start()
    units, unit_cols, depth = mine_ref.shape
    channels = depth // STEP
    n_tiles = unit_cols // LANES
    unit = unit_cols - M
    per_block = TS // LANES
    rows = TS + M
    ch = lax.axis_index("ch")
    me = lax.axis_index("tm") * n_sub + lax.axis_index("sub")
    own_tile = me * (units * unit // LANES)
    identity = (
        lax.broadcasted_iota(jnp.int32, (depth, depth), 0)
        == lax.broadcasted_iota(jnp.int32, (depth, depth), 1)
    )

    def lag(first_tile, count, scale):
        segment = jnp.concatenate([series_ref[first_tile + k] for k in range(count)], axis=1)
        segment = segment.astype(jnp.float32)
        width = count * LANES
        for l in range(STEP):
            moved = segment if l == 0 else pltpu.roll(segment, width - l, axis=1)
            hankel_ref[l * channels : (l + 1) * channels, :width] = moved.astype(jnp.bfloat16)
        scaled = jnp.where(identity, scale, 0.0).astype(jnp.bfloat16)
        lagged = []
        for at in range(0, width, depth):
            size = min(depth, width - at)
            lagged.append(
                lax.dot_general(
                    scaled[:size, :size] if size == depth else jnp.where(
                        lax.broadcasted_iota(jnp.int32, (size, size), 0)
                        == lax.broadcasted_iota(jnp.int32, (size, size), 1), scale, 0.0
                    ).astype(jnp.bfloat16),
                    hankel_ref[:, at : at + size],
                    (((1,), (1,)), ((), ())),
                    preferred_element_type=jnp.float32,
                ).astype(jnp.bfloat16)
            )
        norms = jnp.broadcast_to(jnp.sum(segment * segment, axis=0, keepdims=True), (8, width))
        shift = 1
        while shift < M:
            norms = norms + pltpu.roll(norms, width - shift, axis=1)
            shift *= 2
        return lagged, norms

    lagged, own_norms = lag(own_tile, units * unit // LANES + 1, 1.0)
    groups = [
        piece[at : at + STEP] for piece in lagged for at in range(0, piece.shape[0], STEP)
    ]
    for u in range(units):
        for q in range(unit_cols // STEP):
            place = ((q % n_tiles) * 8 + q // n_tiles) * STEP
            mine_ref[u, place : place + STEP, :] = groups[u * unit // STEP + q]
        best_ref[u] = jnp.full((8, unit_cols), jnp.inf, jnp.float32)
    lane = lax.broadcasted_iota(jnp.int32, (8, LANES), 1)
    own_at = [((lane // STEP) * n_tiles + t) * STEP + lane % STEP for t in range(n_tiles)]
    sublane = lax.broadcasted_iota(jnp.int32, (8, LANES), 0)

    copy.wait()
    owners = lists_smem.shape[0] * n_sub

    def scan(owner, found):
        for slot in range(SLOTS):
            listed = (owner // n_sub, owner % n_sub, slot)
            row_block, col_block = lists_smem[(*listed, 0)], lists_smem[(*listed, 1)]
            for u in range(units):
                block = (own_tile * LANES + u * unit) // TS
                work_smem[found] = (row_block + col_block - block) * units + u
                hit = (row_block == block) | (col_block == block)
                found = found + hit.astype(jnp.int32)
        return found

    if owners <= 16:
        found = jnp.int32(0)
        for owner in range(owners):
            found = scan(owner, found)
    else:
        found = lax.fori_loop(0, owners, scan, jnp.int32(0))

    def ahead(tiles, at):
        turn = at // n_tiles
        tile = tiles[at % n_tiles]
        return tile if turn == 0 else pltpu.roll(tile, LANES - turn * STEP, axis=1)

    def keep_apart(offset):
        for g in range(0, (TS + M) // STEP, M // STEP):
            for at in range(g * STEP, (g + 1) * STEP, 8):
                for t in range(n_tiles):
                    here = (pl.ds(at, 8), pl.ds(t * LANES, LANES))
                    apart = (sublane + (at + offset)) - own_at[t]
                    products_ref[here] = jnp.where(
                        jnp.abs(apart) < EXCL, jnp.inf, products_ref[here]
                    )

    def reduce(u):
        run = TS // STEP

        def some(turn, low):
            part = turn % (STEP // 8)
            first = (turn // (STEP // 8)) * (run * STEP) + part * 8
            ones, twos, fours = {}, {}, {}
            low = list(low)
            for g in range(run + 7):
                ones[g] = [
                    products_ref[pl.ds(first + g * STEP, 8), t * LANES : (t + 1) * LANES]
                    for t in range(n_tiles)
                ]
                if g >= 1:
                    twos[g - 1] = [
                        ones[g - 1][t] + ahead(ones[g], t + 1) for t in range(n_tiles)
                    ]
                if g >= 3:
                    fours[g - 3] = [
                        twos[g - 3][t] + ahead(twos[g - 1], t + 2) for t in range(n_tiles)
                    ]
                if g >= 7:
                    wide = wide_ref[pl.ds(first + (g - 7) * STEP, 8), :]
                    for t in range(n_tiles):
                        score = fours[g - 7][t] + ahead(fours[g - 3], t + 4) + wide
                        low[t] = jnp.minimum(low[t], score)
            return tuple(low)

        low = tuple(best_ref[u, :, t * LANES : (t + 1) * LANES] for t in range(n_tiles))
        for turn in range(TS // run // STEP * (STEP // 8)):
            low = some(turn, low)
        for t in range(n_tiles):
            best_ref[u, :, t * LANES : (t + 1) * LANES] = low[t]

    def incidence(at, _):
        entry = work_smem[2 * at + ch]
        u = entry % units
        partner = entry // units
        lagged, norms = lag(partner * per_block, rows // LANES, -2.0)
        place = 0
        for piece in lagged:
            lagged_ref[place : place + piece.shape[0], :] = piece
            place += piece.shape[0]
        for k in range(per_block):
            one = jnp.broadcast_to(norms[:1, k * LANES : (k + 1) * LANES], (LANES, LANES))
            wide_ref[k * LANES : (k + 1) * LANES, :] = jnp.transpose(one)
        products_ref[...] = lax.dot_general(
            lagged_ref[...], mine_ref[u], (((1,), (1,)), ((), ())), preferred_element_type=jnp.float32
        )
        offset = partner * TS - (own_tile * LANES + u * unit)
        keep_apart(offset)
        reduce(u)
        return 0

    lax.fori_loop(0, (found + 1 - ch) // 2, incidence, 0)

    group = lane // STEP
    for u in range(units):
        low = jnp.min(best_ref[u], axis=0, keepdims=True)
        tiles = [
            jnp.broadcast_to(low[:, t * LANES : (t + 1) * LANES], (8, LANES)) for t in range(n_tiles)
        ]
        for k in range(unit // LANES):
            natural = None
            for g in range(LANES // STEP):
                q = k * (LANES // STEP) + g
                turn = (g - q // n_tiles) % (LANES // STEP)
                tile = tiles[q % n_tiles]
                tile = tile if turn == 0 else pltpu.roll(tile, turn * STEP, axis=1)
                natural = tile if natural is None else jnp.where(group == g, tile, natural)
            at = u * (unit // LANES) + k
            done = (natural[:1] + own_norms[:1, at * LANES : (at + 1) * LANES]) * (1.0 / DEPTH)
            out_ref[at : at + 1, :] = done


def swap_kernel(mine_ref, theirs_ref, sems):
    other = {"ch": 1 - lax.axis_index("ch")}
    barrier = pltpu.get_barrier_semaphore()
    pl.semaphore_signal(barrier, inc=1, device_id=other, device_id_type=MESH)
    pl.semaphore_wait(barrier, 1)
    copy = pltpu.make_async_remote_copy(
        src_ref=mine_ref,
        dst_ref=theirs_ref,
        send_sem=sems.at[0],
        recv_sem=sems.at[1],
        device_id=other,
        device_id_type=MESH,
    )
    copy.start()
    copy.wait()


def lower_kernel(mine_ref, theirs_ref, out_ref):
    out_ref[...] = jnp.minimum(mine_ref[...], theirs_ref[...])


def body(archive, tail, precision, tile_list):
    n_tm, n_sub = lax.axis_size("tm"), lax.axis_size("sub")
    owners = n_tm * n_sub
    channels, span = archive.shape
    piece = span // n_sub
    unit = min(piece, TS)
    units = piece // unit
    every = 2 * channels
    depth = STEP * every
    most = max(piece, TS) + M
    anywhere = pl.BlockSpec(memory_space=pltpu.HBM)
    inside = pl.BlockSpec(memory_space=pltpu.VMEM)
    series, lists = pl.pallas_call(
        functools.partial(gather_kernel, n_tm, n_sub),
        out_shape=[
            pltpu.VMEM((n_tm * span // LANES + 1, every, LANES), jnp.bfloat16),
            pltpu.VMEM((n_tm, n_sub) + tile_list.shape[2:], jnp.int32),
        ],
        in_specs=[anywhere] * 4,
        out_specs=[inside] * 2,
        scratch_shapes=[
            pltpu.VMEM(tail.shape, jnp.float32),
            pltpu.VMEM(precision.shape, jnp.float32),
            pltpu.VMEM((every, span // 2), jnp.float32),
            pltpu.SemaphoreType.DMA((4,)),
            pltpu.SemaphoreType.DMA((2,)),
            pltpu.SemaphoreType.DMA((n_tm,)),
            pltpu.SemaphoreType.DMA((n_tm,)),
            pltpu.SemaphoreType.DMA((n_tm,)),
            pltpu.SemaphoreType.DMA((n_tm,)),
            pltpu.SemaphoreType.DMA((n_tm,)),
            pltpu.SemaphoreType.DMA((n_tm,)),
            pltpu.SemaphoreType.DMA((n_sub,)),
            pltpu.SemaphoreType.DMA((n_sub,)),
            pltpu.SemaphoreType.REGULAR((n_tm,)),
            pltpu.SemaphoreType.REGULAR((n_sub,)),
        ],
        compiler_params=pltpu.CompilerParams(
            collective_id=0, has_side_effects=True, vmem_limit_bytes=62 * 2**20
        ),
    )(tile_list, archive, tail, precision)
    series = pltpu.with_memory_space_constraint(series, pltpu.VMEM)
    lists = pltpu.with_memory_space_constraint(lists, pltpu.VMEM)
    shape = (piece // LANES, LANES)
    mine = pl.pallas_call(
        functools.partial(match_kernel, n_sub),
        out_shape=pltpu.VMEM(shape, jnp.float32),
        in_specs=[inside] * 2,
        out_specs=inside,
        scratch_shapes=[
            pltpu.SMEM(lists.shape, jnp.int32),
            pltpu.SMEM((owners * SLOTS * units + 1,), jnp.int32),
            pltpu.VMEM((depth, most), jnp.bfloat16),
            pltpu.VMEM((TS + M, depth), jnp.bfloat16),
            pltpu.VMEM((units, unit + M, depth), jnp.bfloat16),
            pltpu.VMEM((TS, LANES), jnp.float32),
            pltpu.VMEM((8, LANES), jnp.float32),
            pltpu.VMEM((TS + M, unit + M), jnp.float32),
            pltpu.VMEM((units, 8, unit + M), jnp.float32),
            pltpu.SemaphoreType.DMA,
        ],
        compiler_params=pltpu.CompilerParams(vmem_limit_bytes=32 * 2**20),
    )(series, lists)
    mine = pltpu.with_memory_space_constraint(mine, pltpu.VMEM)
    theirs = pl.pallas_call(
        swap_kernel,
        out_shape=pltpu.VMEM(shape, jnp.float32),
        in_specs=[inside],
        out_specs=inside,
        scratch_shapes=[pltpu.SemaphoreType.DMA((2,))],
        compiler_params=pltpu.CompilerParams(
            collective_id=1, has_side_effects=True, vmem_limit_bytes=16 * 2**20
        ),
    )(mine)
    theirs = pltpu.with_memory_space_constraint(theirs, pltpu.VMEM)
    out = pl.pallas_call(
        lower_kernel,
        out_shape=jax.ShapeDtypeStruct(shape, jnp.float32),
        in_specs=[inside] * 2,
        out_specs=inside,
        compiler_params=pltpu.CompilerParams(vmem_limit_bytes=16 * 2**20),
    )(mine, theirs)
    return out.reshape(-1)


def solution(mesh):
    placed = (P("ch", ("grp", "tm")), P(None, "grp"), P(), P(("grp", "tm"), "sub", None, None))
    return jax.shard_map(
        body, mesh=mesh, in_specs=placed, out_specs=P(("grp", "tm", "sub")), check_vma=False
    )
```

```python
import functools

import jax
import jax.numpy as jnp
from jax import lax
from jax.experimental import pallas as pl
from jax.experimental.pallas import tpu as pltpu
from jax.sharding import PartitionSpec as P

M = 128
TS = 512
SLOTS = 2
DEPTH = 2048
EXCL = 32
LANES = 128
STEP = 16
JOIN = 2
MESH = pl.DeviceIdType.MESH


def whiten(factor, samples):
    return jnp.dot(
        factor, samples, precision=lax.Precision.HIGHEST, preferred_element_type=jnp.float32
    ).astype(jnp.bfloat16)


def gather_kernel(
    n_tm,
    n_sub,
    tiles_hbm,
    archive_hbm,
    tail_hbm,
    precision_hbm,
    series_ref,
    lists_ref,
    tail_ref,
    precision_ref,
    raw_ref,
    load_sems,
    raw_sems,
    time_send,
    time_recv,
    pair_send,
    pair_recv,
    list_send,
    relay_send,
    list_recv,
    here_sems,
):
    tm, sub, ch = lax.axis_index("tm"), lax.axis_index("sub"), lax.axis_index("ch")
    other = 1 - ch
    owners = n_tm * n_sub
    me = tm * n_sub + sub
    channels, span = archive_hbm.shape
    half = span // 2
    tiles = half // LANES
    last = n_tm * span // LANES

    def send(source, target, sem, landed, device):
        return pltpu.make_async_remote_copy(
            src_ref=source,
            dst_ref=target,
            send_sem=sem,
            recv_sem=landed,
            device_id=device,
            device_id_type=MESH,
        )

    def each_owner(action):
        if owners <= 16:
            for rank in range(owners):
                action(rank, rank // n_sub, rank % n_sub)
        else:
            lax.fori_loop(
                0, owners, lambda rank, _: (action(rank, rank // n_sub, rank % n_sub), 0)[1], 0
            )

    def above(rank, t, s):
        return (t >= tm) & (s >= sub) & (rank != me)

    def below(rank, t, s):
        return (t <= tm) & (s <= sub) & (rank != me)

    barrier = pltpu.get_barrier_semaphore()
    pl.semaphore_signal(barrier, inc=1, device_id={"ch": other}, device_id_type=MESH)

    def announce(rank, t, s):
        @pl.when(above(rank, t, s))
        def _():
            pl.semaphore_signal(
                barrier, inc=1, device_id={"tm": t, "sub": s}, device_id_type=MESH
            )

    each_owner(announce)
    own_rows = pl.ds(pl.multiple_of(ch * channels, channels), channels)
    own_half = archive_hbm.at[:, pl.ds(pl.multiple_of(ch * half, half), half)]
    own_list = lists_ref.at[me]
    loads = [
        pltpu.make_async_copy(source, target, load_sems.at[at])
        for at, (source, target) in enumerate(
            (
                (precision_hbm, precision_ref),
                (tail_hbm, tail_ref),
                (own_half, raw_ref.at[own_rows, :]),
                (tiles_hbm.at[0, 0], own_list),
            )
        )
    ]
    for load in loads:
        load.start()
    pl.semaphore_wait(barrier, (tm + 1) * (sub + 1))

    swap = send(
        archive_hbm.at[:, pl.ds(pl.multiple_of(other * half, half), half)],
        raw_ref.at[own_rows, :],
        raw_sems.at[0],
        raw_sems.at[1],
        {"ch": other},
    )
    swap.start()

    def direct(rank, t, s):
        return send(
            tiles_hbm.at[0, 0],
            own_list,
            list_send.at[rank],
            list_recv.at[me],
            {"tm": t, "sub": s},
        )

    def answer(rank, t, s):
        @pl.when(below(rank, t, s))
        def _():
            pl.semaphore_signal(
                here_sems.at[me], inc=1, device_id={"tm": t, "sub": s}, device_id_type=MESH
            )
            direct(rank, t, s).start()

    each_owner(answer)
    for load in loads[:2]:
        load.wait()
    factor = precision_ref[...]
    series_ref[last] = jnp.zeros((2 * channels, LANES), jnp.bfloat16)
    series_ref[last, :, : M - 1] = whiten(factor, tail_ref[...])
    for load in loads[2:]:
        load.wait()
    swap.wait_recv()

    def chunk(owner, part):
        return series_ref.at[pl.ds((owner * 2 + part) * tiles, tiles)]

    mine = chunk(tm, ch)
    whitened = whiten(factor, raw_ref[...])
    for k in range(tiles):
        series_ref[(tm * 2 + ch) * tiles + k] = whitened[:, k * LANES : (k + 1) * LANES]

    def along_time(t):
        return send(mine, mine, time_send.at[t], time_recv.at[tm], {"tm": t})

    to_pair = []

    def forward(held):
        step = len(to_pair)
        copy = send(held, held, pair_send.at[step], pair_recv.at[step], {"ch": other})
        to_pair.append(copy)
        copy.start()

    for t in range(n_tm):
        pl.when(t < tm)(along_time(t).start)
    forward(mine)
    for t in range(1, n_tm):

        @pl.when(t > tm)
        def _():
            pl.semaphore_wait(here_sems.at[t * n_sub + sub], 1)
            along_time(t).start()
            direct(t * n_sub + sub, t, sub).start()

    def list_up(rank, t, s):
        @pl.when(above(rank, t, s) & (s != sub))
        def _():
            pl.semaphore_wait(here_sems.at[rank], 1)
            direct(rank, t, s).start()

    each_owner(list_up)

    def landed(rank):
        held = lists_ref.at[rank]
        return send(held, held, list_send.at[0], list_recv.at[rank], {"ch": other})

    def relay(rank, t, s):
        held = lists_ref.at[tm * n_sub + s]
        return send(
            held, held, relay_send.at[rank], list_recv.at[tm * n_sub + s], {"tm": t, "sub": sub}
        )

    def relayed(t, s):
        return ((s < sub) & (t < tm)) | ((s > sub) & (t > tm))

    for s in range(n_sub):
        pl.when(s != sub)(landed(tm * n_sub + s).wait_recv)
    each_owner(lambda rank, t, s: pl.when(relayed(t, s))(relay(rank, t, s).start))

    for step in range(1, n_tm):
        source = step + ((tm + n_tm - step) // n_tm) * (tm - 2 * step)
        held = chunk(source, ch)
        send(held, held, time_send.at[0], time_recv.at[source], {"ch": other}).wait_recv()
        forward(held)
    for copy in to_pair:
        copy.wait_recv()
    each_owner(lambda rank, t, s: pl.when(t != tm)(landed(rank).wait_recv))

    swap.wait_send()
    for copy in to_pair:
        copy.wait_send()
    for t in range(n_tm):
        pl.when(t != tm)(along_time(t).wait_send)
    each_owner(
        lambda rank, t, s: pl.when(above(rank, t, s) | below(rank, t, s))(direct(rank, t, s).wait_send)
    )
    each_owner(lambda rank, t, s: pl.when(relayed(t, s))(relay(rank, t, s).wait_send))


def match_kernel(
    n_sub,
    series_ref,
    lists_ref,
    out_ref,
    lists_smem,
    work_smem,
    hankel_ref,
    lagged_ref,
    mine_ref,
    wide_ref,
    near_ref,
    products_ref,
    best_ref,
    list_sem,
):
    copy = pltpu.make_async_copy(lists_ref, lists_smem, list_sem)
    copy.start()
    units, unit_cols, _ = mine_ref.shape
    depth = hankel_ref.shape[0]
    channels = depth // STEP
    n_tiles = unit_cols // LANES
    unit = unit_cols - M
    per_block = TS // LANES
    rows = TS + M
    ch = lax.axis_index("ch")
    me = lax.axis_index("tm") * n_sub + lax.axis_index("sub")
    own_tile = me * (units * unit // LANES)
    def lag(first_tile, count, scale):
        pieces = [series_ref[first_tile + k].astype(jnp.float32) for k in range(count)]
        segment = jnp.concatenate(pieces, axis=1)
        width = count * LANES
        column = lax.broadcasted_iota(jnp.int32, (channels, LANES), 1)
        turned = {}

        def turn(k, l):
            k = min(k, count - 1)
            if (k, l) not in turned:
                turned[k, l] = pieces[k] if l == 0 else pltpu.roll(pieces[k], LANES - l, axis=1)
            return turned[k, l]

        def moved(k, l):
            here = turn(k, l)
            here = here if l == 0 else jnp.where(column < LANES - l, here, turn(k + 1, l))
            return here.astype(jnp.bfloat16)

        lagged = []
        for at in range(0, count, 2):
            tiles = range(at, min(at + 2, count))
            size = len(tiles) * LANES
            hankel = jnp.concatenate(
                [jnp.concatenate([moved(k, l) for k in tiles], axis=1) for l in range(STEP)], axis=0
            )
            unit_matrix = jnp.where(
                lax.broadcasted_iota(jnp.int32, (size, size), 0)
                == lax.broadcasted_iota(jnp.int32, (size, size), 1),
                scale,
                0.0,
            ).astype(jnp.bfloat16)
            lagged.append(
                lax.dot_general(
                    unit_matrix, hankel, (((1,), (1,)), ((), ())), preferred_element_type=jnp.float32
                ).astype(jnp.bfloat16)
            )
        norms = jnp.broadcast_to(jnp.sum(segment * segment, axis=0, keepdims=True), (8, width))
        shift = 1
        while shift < M:
            norms = norms + pltpu.roll(norms, width - shift, axis=1)
            shift *= 2
        return lagged, norms

    lagged, own_norms = lag(own_tile, units * unit // LANES + 1, 1.0)
    groups = [
        piece[at : at + STEP] for piece in lagged for at in range(0, piece.shape[0], STEP)
    ]
    for u in range(units):
        for q in range(unit_cols // STEP):
            place = ((q % n_tiles) * 8 + q // n_tiles) * STEP
            for v in range(JOIN):
                at = min(u * unit // STEP + q + v, len(groups) - 1)
                mine_ref[u, place : place + STEP, v * depth : (v + 1) * depth] = groups[at]
        best_ref[u] = jnp.full((8, unit_cols), jnp.inf, jnp.float32)
    lane = lax.broadcasted_iota(jnp.int32, (8, LANES), 1)
    own_at = [((lane // STEP) * n_tiles + t) * STEP + lane % STEP for t in range(n_tiles)]
    sublane = lax.broadcasted_iota(jnp.int32, (8, LANES), 0)

    copy.wait()
    owners = lists_smem.shape[0]

    def scan(owner, found):
        for slot in range(SLOTS):
            row_block, col_block = lists_smem[owner, slot, 0], lists_smem[owner, slot, 1]
            for u in range(units):
                block = (own_tile * LANES + u * unit) // TS
                work_smem[found] = (row_block + col_block - block) * units + u
                hit = (row_block == block) | (col_block == block)
                found = found + hit.astype(jnp.int32)
        return found

    if owners <= 16:
        found = jnp.int32(0)
        for owner in range(owners):
            found = scan(owner, found)
    else:
        found = lax.fori_loop(0, owners, scan, jnp.int32(0))

    def ahead(tiles, at):
        turn = at // n_tiles
        tile = tiles[at % n_tiles]
        return tile if turn == 0 else pltpu.roll(tile, LANES - turn * STEP, axis=1)

    def keep_apart(offset):
        for g in range(products_ref.shape[0] // STEP):
            if g % (M // STEP) < JOIN:
                for at in range(g * STEP, (g + 1) * STEP, 8):
                    for t in range(n_tiles):
                        here = (pl.ds(at, 8), pl.ds(t * LANES, LANES))
                        apart = (sublane + (at + offset)) - own_at[t]
                        products_ref[here] = jnp.where(
                            jnp.abs(apart) < EXCL, jnp.inf, products_ref[here]
                        )

    def reduce(u):
        low = [best_ref[u, :, t * LANES : (t + 1) * LANES] for t in range(n_tiles)]
        for part in range(0, STEP, 8):
            sums = {}
            for g in range(products_ref.shape[0] // STEP):
                at = g * STEP + part
                sums[JOIN, g] = [
                    products_ref[at : at + 8, t * LANES : (t + 1) * LANES] for t in range(n_tiles)
                ]
                first, size = g, JOIN
                while size < M // STEP and first >= size:
                    first -= size
                    early, late = sums[size, first], sums[size, first + size]
                    sums[2 * size, first] = [
                        early[t] + ahead(late, t + size) for t in range(n_tiles)
                    ]
                    size *= 2
                if size == M // STEP:
                    at = first * STEP + part
                    wide = wide_ref[at : at + 8, :]
                    for t in range(n_tiles):
                        low[t] = jnp.minimum(low[t], sums[size, first][t] + wide)
        for t in range(n_tiles):
            best_ref[u, :, t * LANES : (t + 1) * LANES] = low[t]

    def incidence(at, _):
        entry = work_smem[2 * at + ch]
        u = entry % units
        partner = entry // units
        lagged, norms = lag(partner * per_block, rows // LANES, -2.0)
        place = 0
        for piece in lagged:
            lagged_ref[place : place + piece.shape[0], :] = piece
            place += piece.shape[0]
        for k in range(per_block):
            one = jnp.broadcast_to(norms[:1, k * LANES : (k + 1) * LANES], (LANES, LANES))
            wide_ref[k * LANES : (k + 1) * LANES, :] = jnp.transpose(one)
        longer = [lagged_ref[v * STEP : v * STEP + products_ref.shape[0], :] for v in range(JOIN)]
        products_ref[...] = lax.dot_general(
            jnp.concatenate(longer, axis=1) if JOIN > 1 else longer[0],
            mine_ref[u],
            (((1,), (1,)), ((), ())),
            preferred_element_type=jnp.float32,
        )
        offset = partner * TS - (own_tile * LANES + u * unit)
        keep_apart(offset)
        reduce(u)
        return 0

    lax.fori_loop(0, (found + 1 - ch) // 2, incidence, 0)

    group = lane // STEP
    for u in range(units):
        low = jnp.min(best_ref[u], axis=0, keepdims=True)
        tiles = [
            jnp.broadcast_to(low[:, t * LANES : (t + 1) * LANES], (8, LANES)) for t in range(n_tiles)
        ]
        for k in range(unit // LANES):
            natural = None
            for g in range(LANES // STEP):
                q = k * (LANES // STEP) + g
                turn = (g - q // n_tiles) % (LANES // STEP)
                tile = tiles[q % n_tiles]
                tile = tile if turn == 0 else pltpu.roll(tile, turn * STEP, axis=1)
                natural = tile if natural is None else jnp.where(group == g, tile, natural)
            at = u * (unit // LANES) + k
            done = (natural[:1] + own_norms[:1, at * LANES : (at + 1) * LANES]) * (1.0 / DEPTH)
            out_ref[at : at + 1, :] = done


def swap_kernel(mine_ref, theirs_ref, sems):
    other = {"ch": 1 - lax.axis_index("ch")}
    barrier = pltpu.get_barrier_semaphore()
    pl.semaphore_signal(barrier, inc=1, device_id=other, device_id_type=MESH)
    pl.semaphore_wait(barrier, 1)
    copy = pltpu.make_async_remote_copy(
        src_ref=mine_ref,
        dst_ref=theirs_ref,
        send_sem=sems.at[0],
        recv_sem=sems.at[1],
        device_id=other,
        device_id_type=MESH,
    )
    copy.start()
    copy.wait()


def lower_kernel(mine_ref, theirs_ref, out_ref):
    out_ref[...] = jnp.minimum(mine_ref[...], theirs_ref[...])


def body(archive, tail, precision, tile_list):
    n_tm, n_sub = lax.axis_size("tm"), lax.axis_size("sub")
    owners = n_tm * n_sub
    channels, span = archive.shape
    piece = span // n_sub
    unit = min(piece, TS)
    units = piece // unit
    every = 2 * channels
    depth = STEP * every
    most = max(piece, TS) + M
    anywhere = pl.BlockSpec(memory_space=pltpu.HBM)
    inside = pl.BlockSpec(memory_space=pltpu.VMEM)
    series, lists = pl.pallas_call(
        functools.partial(gather_kernel, n_tm, n_sub),
        out_shape=[
            pltpu.VMEM((n_tm * span // LANES + 1, every, LANES), jnp.bfloat16),
            pltpu.VMEM((owners,) + tile_list.shape[2:], jnp.int32),
        ],
        in_specs=[anywhere] * 4,
        out_specs=[inside] * 2,
        scratch_shapes=[
            pltpu.VMEM(tail.shape, jnp.float32),
            pltpu.VMEM(precision.shape, jnp.float32),
            pltpu.VMEM((every, span // 2), jnp.float32),
            pltpu.SemaphoreType.DMA((4,)),
            pltpu.SemaphoreType.DMA((2,)),
            pltpu.SemaphoreType.DMA((n_tm,)),
            pltpu.SemaphoreType.DMA((n_tm,)),
            pltpu.SemaphoreType.DMA((n_tm,)),
            pltpu.SemaphoreType.DMA((n_tm,)),
            pltpu.SemaphoreType.DMA((owners,)),
            pltpu.SemaphoreType.DMA((owners,)),
            pltpu.SemaphoreType.DMA((owners,)),
            pltpu.SemaphoreType.REGULAR((owners,)),
        ],
        compiler_params=pltpu.CompilerParams(
            collective_id=0, has_side_effects=True, vmem_limit_bytes=62 * 2**20
        ),
    )(tile_list, archive, tail, precision)
    series = pltpu.with_memory_space_constraint(series, pltpu.VMEM)
    lists = pltpu.with_memory_space_constraint(lists, pltpu.VMEM)
    shape = (piece // LANES, LANES)
    mine = pl.pallas_call(
        functools.partial(match_kernel, n_sub),
        out_shape=pltpu.VMEM(shape, jnp.float32),
        in_specs=[inside] * 2,
        out_specs=inside,
        scratch_shapes=[
            pltpu.SMEM(lists.shape, jnp.int32),
            pltpu.SMEM((owners * SLOTS * units + 1,), jnp.int32),
            pltpu.VMEM((depth, most), jnp.bfloat16),
            pltpu.VMEM((TS + M, depth), jnp.bfloat16),
            pltpu.VMEM((units, unit + M, JOIN * depth), jnp.bfloat16),
            pltpu.VMEM((TS, LANES), jnp.float32),
            pltpu.VMEM((8, LANES), jnp.float32),
            pltpu.VMEM((TS + M - JOIN * STEP, unit + M), jnp.float32),
            pltpu.VMEM((units, 8, unit + M), jnp.float32),
            pltpu.SemaphoreType.DMA,
        ],
        compiler_params=pltpu.CompilerParams(vmem_limit_bytes=32 * 2**20),
    )(series, lists)
    mine = pltpu.with_memory_space_constraint(mine, pltpu.VMEM)
    theirs = pl.pallas_call(
        swap_kernel,
        out_shape=pltpu.VMEM(shape, jnp.float32),
        in_specs=[inside],
        out_specs=inside,
        scratch_shapes=[pltpu.SemaphoreType.DMA((2,))],
        compiler_params=pltpu.CompilerParams(
            collective_id=1, has_side_effects=True, vmem_limit_bytes=16 * 2**20
        ),
    )(mine)
    theirs = pltpu.with_memory_space_constraint(theirs, pltpu.VMEM)
    out = pl.pallas_call(
        lower_kernel,
        out_shape=jax.ShapeDtypeStruct(shape, jnp.float32),
        in_specs=[inside] * 2,
        out_specs=inside,
        compiler_params=pltpu.CompilerParams(vmem_limit_bytes=16 * 2**20),
    )(mine, theirs)
    return out.reshape(-1)


def solution(mesh):
    placed = (P("ch", ("grp", "tm")), P(None, "grp"), P(), P(("grp", "tm"), "sub", None, None))
    return jax.shard_map(
        body, mesh=mesh, in_specs=placed, out_specs=P(("grp", "tm", "sub")), check_vma=False
    )
```

```python
import functools

import jax
import jax.numpy as jnp
from jax import lax
from jax.experimental import pallas as pl
from jax.experimental.pallas import tpu as pltpu
from jax.sharding import PartitionSpec as P

M = 128
TS = 512
SLOTS = 2
DEPTH = 2048
EXCL = 32
LANES = 128
STEP = 16
JOIN = 2
MESH = pl.DeviceIdType.MESH


def whiten(factor, samples):
    return jnp.dot(
        factor, samples, precision=lax.Precision.HIGHEST, preferred_element_type=jnp.float32
    ).astype(jnp.bfloat16)


def lag(series_ref, first_tile, count, scale):
    channels = series_ref.shape[1]
    pieces = [series_ref[first_tile + k].astype(jnp.float32) for k in range(count)]
    segment = jnp.concatenate(pieces, axis=1)
    width = count * LANES
    column = lax.broadcasted_iota(jnp.int32, (channels, LANES), 1)
    turned = {}

    def turn(k, l):
        k = min(k, count - 1)
        if (k, l) not in turned:
            turned[k, l] = pieces[k] if l == 0 else pltpu.roll(pieces[k], LANES - l, axis=1)
        return turned[k, l]

    def moved(k, l):
        here = turn(k, l)
        here = here if l == 0 else jnp.where(column < LANES - l, here, turn(k + 1, l))
        return here.astype(jnp.bfloat16)

    lagged = []
    for at in range(0, count, 2):
        tiles = range(at, min(at + 2, count))
        size = len(tiles) * LANES
        hankel = jnp.concatenate(
            [jnp.concatenate([moved(k, l) for k in tiles], axis=1) for l in range(STEP)], axis=0
        )
        unit_matrix = jnp.where(
            lax.broadcasted_iota(jnp.int32, (size, size), 0)
            == lax.broadcasted_iota(jnp.int32, (size, size), 1),
            scale,
            0.0,
        ).astype(jnp.bfloat16)
        lagged.append(
            lax.dot_general(
                unit_matrix, hankel, (((1,), (1,)), ((), ())), preferred_element_type=jnp.float32
            ).astype(jnp.bfloat16)
        )
    norms = jnp.broadcast_to(jnp.sum(segment * segment, axis=0, keepdims=True), (8, width))
    shift = 1
    while shift < M:
        norms = norms + pltpu.roll(norms, width - shift, axis=1)
        shift *= 2
    return lagged, norms


def own_columns(series_ref, own_tile, mine_ref, norms_ref):
    units, unit_cols, joined = mine_ref.shape
    depth = joined // JOIN
    n_tiles = unit_cols // LANES
    unit = unit_cols - M
    lagged, norms_ref[...] = lag(series_ref, own_tile, units * unit // LANES + 1, 1.0)
    groups = [piece[at : at + STEP] for piece in lagged for at in range(0, piece.shape[0], STEP)]
    for u in range(units):
        for q in range(unit_cols // STEP):
            place = ((q % n_tiles) * 8 + q // n_tiles) * STEP
            for v in range(JOIN):
                at = min(u * unit // STEP + q + v, len(groups) - 1)
                mine_ref[u, place : place + STEP, v * depth : (v + 1) * depth] = groups[at]


def gather_kernel(
    n_tm,
    n_sub,
    tiles_hbm,
    archive_hbm,
    tail_hbm,
    precision_hbm,
    series_ref,
    lists_smem,
    mine_ref,
    norms_ref,
    lists_ref,
    tail_ref,
    precision_ref,
    raw_ref,
    load_sems,
    raw_sems,
    time_send,
    time_recv,
    pair_send,
    pair_recv,
    list_send,
    relay_send,
    list_recv,
    here_sems,
):
    tm, sub, ch = lax.axis_index("tm"), lax.axis_index("sub"), lax.axis_index("ch")
    other = 1 - ch
    owners = n_tm * n_sub
    me = tm * n_sub + sub
    channels, span = archive_hbm.shape
    half = span // 2
    tiles = half // LANES
    last = n_tm * span // LANES

    def send(source, target, sem, landed, device):
        return pltpu.make_async_remote_copy(
            src_ref=source,
            dst_ref=target,
            send_sem=sem,
            recv_sem=landed,
            device_id=device,
            device_id_type=MESH,
        )

    def each_owner(action):
        if owners <= 16:
            for rank in range(owners):
                action(rank, rank // n_sub, rank % n_sub)
        else:
            lax.fori_loop(
                0, owners, lambda rank, _: (action(rank, rank // n_sub, rank % n_sub), 0)[1], 0
            )

    def above(rank, t, s):
        return (t >= tm) & (s >= sub) & (rank != me)

    def below(rank, t, s):
        return (t <= tm) & (s <= sub) & (rank != me)

    barrier = pltpu.get_barrier_semaphore()
    pl.semaphore_signal(barrier, inc=1, device_id={"ch": other}, device_id_type=MESH)

    def announce(rank, t, s):
        @pl.when(above(rank, t, s))
        def _():
            pl.semaphore_signal(
                barrier, inc=1, device_id={"tm": t, "sub": s}, device_id_type=MESH
            )

    each_owner(announce)
    own_rows = pl.ds(pl.multiple_of(ch * channels, channels), channels)
    own_half = archive_hbm.at[:, pl.ds(pl.multiple_of(ch * half, half), half)]
    own_list = lists_ref.at[me]
    loads = [
        pltpu.make_async_copy(source, target, load_sems.at[at])
        for at, (source, target) in enumerate(
            (
                (precision_hbm, precision_ref),
                (tail_hbm, tail_ref),
                (own_half, raw_ref.at[own_rows, :]),
                (tiles_hbm.at[0, 0], own_list),
            )
        )
    ]
    for load in loads:
        load.start()
    pl.semaphore_wait(barrier, (tm + 1) * (sub + 1))

    swap = send(
        archive_hbm.at[:, pl.ds(pl.multiple_of(other * half, half), half)],
        raw_ref.at[own_rows, :],
        raw_sems.at[0],
        raw_sems.at[1],
        {"ch": other},
    )
    swap.start()

    def direct(rank, t, s):
        return send(
            tiles_hbm.at[0, 0],
            own_list,
            list_send.at[rank],
            list_recv.at[me],
            {"tm": t, "sub": s},
        )

    def answer(rank, t, s):
        @pl.when(below(rank, t, s))
        def _():
            pl.semaphore_signal(
                here_sems.at[me], inc=1, device_id={"tm": t, "sub": s}, device_id_type=MESH
            )
            direct(rank, t, s).start()

    each_owner(answer)
    for load in loads[:2]:
        load.wait()
    factor = precision_ref[...]
    series_ref[last] = jnp.zeros((2 * channels, LANES), jnp.bfloat16)
    series_ref[last, :, : M - 1] = whiten(factor, tail_ref[...])
    for load in loads[2:]:
        load.wait()
    swap.wait_recv()

    def chunk(owner, part):
        return series_ref.at[pl.ds((owner * 2 + part) * tiles, tiles)]

    mine = chunk(tm, ch)
    whitened = whiten(factor, raw_ref[...])
    for k in range(tiles):
        series_ref[(tm * 2 + ch) * tiles + k] = whitened[:, k * LANES : (k + 1) * LANES]

    def along_time(t):
        return send(mine, mine, time_send.at[t], time_recv.at[tm], {"tm": t})

    to_pair = []

    def forward(held):
        step = len(to_pair)
        copy = send(held, held, pair_send.at[step], pair_recv.at[step], {"ch": other})
        to_pair.append(copy)
        copy.start()

    for t in range(n_tm):
        pl.when(t < tm)(along_time(t).start)
    forward(mine)
    for t in range(1, n_tm):

        @pl.when(t > tm)
        def _():
            pl.semaphore_wait(here_sems.at[t * n_sub + sub], 1)
            along_time(t).start()
            direct(t * n_sub + sub, t, sub).start()

    def list_up(rank, t, s):
        @pl.when(above(rank, t, s) & (s != sub))
        def _():
            pl.semaphore_wait(here_sems.at[rank], 1)
            direct(rank, t, s).start()

    each_owner(list_up)

    def landed(rank):
        held = lists_ref.at[rank]
        return send(held, held, list_send.at[0], list_recv.at[rank], {"ch": other})

    def relay(rank, t, s):
        held = lists_ref.at[tm * n_sub + s]
        return send(
            held, held, relay_send.at[rank], list_recv.at[tm * n_sub + s], {"tm": t, "sub": sub}
        )

    def relayed(t, s):
        return ((s < sub) & (t < tm)) | ((s > sub) & (t > tm))

    for s in range(n_sub):
        pl.when(s != sub)(landed(tm * n_sub + s).wait_recv)
    each_owner(lambda rank, t, s: pl.when(relayed(t, s))(relay(rank, t, s).start))

    own_tile = me * (span // n_sub // LANES)
    early = (sub != n_sub - 1) | (tm == 0) | (tm == n_tm - 1)

    def prepare():
        own_columns(series_ref, own_tile, mine_ref, norms_ref)

    for step in range(1, n_tm):
        source = step + ((tm + n_tm - step) // n_tm) * (tm - 2 * step)
        held = chunk(source, ch)
        send(held, held, time_send.at[0], time_recv.at[source], {"ch": other}).wait_recv()
        forward(held)
        if step == 1:
            for copy in to_pair:
                copy.wait_recv()
            pl.when(early)(prepare)
    each_owner(lambda rank, t, s: pl.when(t != tm)(landed(rank).wait_recv))
    keep = pltpu.make_async_copy(lists_ref, lists_smem, load_sems.at[0])
    keep.start()
    for copy in to_pair[2:]:
        copy.wait_recv()
    pl.when(jnp.logical_not(early))(prepare)
    keep.wait()

    swap.wait_send()
    for copy in to_pair:
        copy.wait_send()
    for t in range(n_tm):
        pl.when(t != tm)(along_time(t).wait_send)
    each_owner(
        lambda rank, t, s: pl.when(above(rank, t, s) | below(rank, t, s))(direct(rank, t, s).wait_send)
    )
    each_owner(lambda rank, t, s: pl.when(relayed(t, s))(relay(rank, t, s).wait_send))


def match_kernel(
    n_sub,
    series_ref,
    lists_smem,
    mine_ref,
    norms_ref,
    out_ref,
    work_smem,
    lagged_ref,
    wide_ref,
    products_ref,
    best_ref,
):
    units, unit_cols, _ = mine_ref.shape
    n_tiles = unit_cols // LANES
    unit = unit_cols - M
    per_block = TS // LANES
    rows = TS + M
    ch = lax.axis_index("ch")
    me = lax.axis_index("tm") * n_sub + lax.axis_index("sub")
    own_tile = me * (units * unit // LANES)
    for u in range(units):
        best_ref[u] = jnp.full((8, unit_cols), jnp.inf, jnp.float32)
    lane = lax.broadcasted_iota(jnp.int32, (8, LANES), 1)
    own_at = [((lane // STEP) * n_tiles + t) * STEP + lane % STEP for t in range(n_tiles)]
    sublane = lax.broadcasted_iota(jnp.int32, (8, LANES), 0)

    owners = lists_smem.shape[0]

    def scan(owner, found):
        for slot in range(SLOTS):
            row_block, col_block = lists_smem[owner, slot, 0], lists_smem[owner, slot, 1]
            for u in range(units):
                block = (own_tile * LANES + u * unit) // TS
                work_smem[found] = (row_block + col_block - block) * units + u
                hit = (row_block == block) | (col_block == block)
                found = found + hit.astype(jnp.int32)
        return found

    if owners <= 16:
        found = jnp.int32(0)
        for owner in range(owners):
            found = scan(owner, found)
    else:
        found = lax.fori_loop(0, owners, scan, jnp.int32(0))

    def ahead(tiles, at):
        turn = at // n_tiles
        tile = tiles[at % n_tiles]
        return tile if turn == 0 else pltpu.roll(tile, LANES - turn * STEP, axis=1)

    def keep_apart(offset):
        for g in range(products_ref.shape[0] // STEP):
            if g % (M // STEP) < JOIN:
                for at in range(g * STEP, (g + 1) * STEP, 8):
                    for t in range(n_tiles):
                        here = (pl.ds(at, 8), pl.ds(t * LANES, LANES))
                        apart = (sublane + (at + offset)) - own_at[t]
                        products_ref[here] = jnp.where(
                            jnp.abs(apart) < EXCL, jnp.inf, products_ref[here]
                        )

    def reduce(u):
        low = [best_ref[u, :, t * LANES : (t + 1) * LANES] for t in range(n_tiles)]
        for part in range(0, STEP, 8):
            sums = {}
            for g in range(products_ref.shape[0] // STEP):
                at = g * STEP + part
                sums[JOIN, g] = [
                    products_ref[at : at + 8, t * LANES : (t + 1) * LANES] for t in range(n_tiles)
                ]
                first, size = g, JOIN
                while size < M // STEP and first >= size:
                    first -= size
                    early, late = sums[size, first], sums[size, first + size]
                    sums[2 * size, first] = [
                        early[t] + ahead(late, t + size) for t in range(n_tiles)
                    ]
                    size *= 2
                if size == M // STEP:
                    at = first * STEP + part
                    wide = wide_ref[at : at + 8, :]
                    for t in range(n_tiles):
                        low[t] = jnp.minimum(low[t], sums[size, first][t] + wide)
        for t in range(n_tiles):
            best_ref[u, :, t * LANES : (t + 1) * LANES] = low[t]

    def incidence(at, _):
        entry = work_smem[2 * at + ch]
        u = entry % units
        partner = entry // units
        lagged, norms = lag(series_ref, partner * per_block, rows // LANES, -2.0)
        place = 0
        for piece in lagged:
            lagged_ref[place : place + piece.shape[0], :] = piece
            place += piece.shape[0]
        for k in range(per_block):
            one = jnp.broadcast_to(norms[:1, k * LANES : (k + 1) * LANES], (LANES, LANES))
            wide_ref[k * LANES : (k + 1) * LANES, :] = jnp.transpose(one)
        longer = [lagged_ref[v * STEP : v * STEP + products_ref.shape[0], :] for v in range(JOIN)]
        products_ref[...] = lax.dot_general(
            jnp.concatenate(longer, axis=1) if JOIN > 1 else longer[0],
            mine_ref[u],
            (((1,), (1,)), ((), ())),
            preferred_element_type=jnp.float32,
        )
        offset = partner * TS - (own_tile * LANES + u * unit)
        keep_apart(offset)
        reduce(u)
        return 0

    lax.fori_loop(0, (found + 1 - ch) // 2, incidence, 0)

    group = lane // STEP
    for u in range(units):
        low = jnp.min(best_ref[u], axis=0, keepdims=True)
        tiles = [
            jnp.broadcast_to(low[:, t * LANES : (t + 1) * LANES], (8, LANES)) for t in range(n_tiles)
        ]
        for k in range(unit // LANES):
            natural = None
            for g in range(LANES // STEP):
                q = k * (LANES // STEP) + g
                turn = (g - q // n_tiles) % (LANES // STEP)
                tile = tiles[q % n_tiles]
                tile = tile if turn == 0 else pltpu.roll(tile, turn * STEP, axis=1)
                natural = tile if natural is None else jnp.where(group == g, tile, natural)
            at = u * (unit // LANES) + k
            done = (natural[:1] + norms_ref[:1, at * LANES : (at + 1) * LANES]) * (1.0 / DEPTH)
            out_ref[at : at + 1, :] = done


def swap_kernel(mine_ref, theirs_ref, sems):
    other = {"ch": 1 - lax.axis_index("ch")}
    barrier = pltpu.get_barrier_semaphore()
    pl.semaphore_signal(barrier, inc=1, device_id=other, device_id_type=MESH)
    pl.semaphore_wait(barrier, 1)
    copy = pltpu.make_async_remote_copy(
        src_ref=mine_ref,
        dst_ref=theirs_ref,
        send_sem=sems.at[0],
        recv_sem=sems.at[1],
        device_id=other,
        device_id_type=MESH,
    )
    copy.start()
    copy.wait()


def lower_kernel(mine_ref, theirs_ref, out_ref):
    out_ref[...] = jnp.minimum(mine_ref[...], theirs_ref[...])


def body(archive, tail, precision, tile_list):
    n_tm, n_sub = lax.axis_size("tm"), lax.axis_size("sub")
    owners = n_tm * n_sub
    channels, span = archive.shape
    piece = span // n_sub
    unit = min(piece, TS)
    units = piece // unit
    every = 2 * channels
    depth = STEP * every
    anywhere = pl.BlockSpec(memory_space=pltpu.HBM)
    inside = pl.BlockSpec(memory_space=pltpu.VMEM)
    scalars = pl.BlockSpec(memory_space=pltpu.SMEM)
    series, lists, own, norms = pl.pallas_call(
        functools.partial(gather_kernel, n_tm, n_sub),
        out_shape=[
            pltpu.VMEM((n_tm * span // LANES + 1, every, LANES), jnp.bfloat16),
            pltpu.SMEM((owners,) + tile_list.shape[2:], jnp.int32),
            pltpu.VMEM((units, unit + M, JOIN * depth), jnp.bfloat16),
            pltpu.VMEM((8, piece + M), jnp.float32),
        ],
        in_specs=[anywhere] * 4,
        out_specs=[inside, scalars, inside, inside],
        scratch_shapes=[
            pltpu.VMEM((owners,) + tile_list.shape[2:], jnp.int32),
            pltpu.VMEM(tail.shape, jnp.float32),
            pltpu.VMEM(precision.shape, jnp.float32),
            pltpu.VMEM((every, span // 2), jnp.float32),
            pltpu.SemaphoreType.DMA((4,)),
            pltpu.SemaphoreType.DMA((2,)),
            pltpu.SemaphoreType.DMA((n_tm,)),
            pltpu.SemaphoreType.DMA((n_tm,)),
            pltpu.SemaphoreType.DMA((n_tm,)),
            pltpu.SemaphoreType.DMA((n_tm,)),
            pltpu.SemaphoreType.DMA((owners,)),
            pltpu.SemaphoreType.DMA((owners,)),
            pltpu.SemaphoreType.DMA((owners,)),
            pltpu.SemaphoreType.REGULAR((owners,)),
        ],
        compiler_params=pltpu.CompilerParams(
            collective_id=0, has_side_effects=True, vmem_limit_bytes=62 * 2**20
        ),
    )(tile_list, archive, tail, precision)
    series, own, norms = [
        pltpu.with_memory_space_constraint(array, pltpu.VMEM) for array in (series, own, norms)
    ]
    lists = pltpu.with_memory_space_constraint(lists, pltpu.SMEM)
    shape = (piece // LANES, LANES)
    mine = pl.pallas_call(
        functools.partial(match_kernel, n_sub),
        out_shape=pltpu.VMEM(shape, jnp.float32),
        in_specs=[inside, scalars, inside, inside],
        out_specs=inside,
        scratch_shapes=[
            pltpu.SMEM((owners * SLOTS * units + 1,), jnp.int32),
            pltpu.VMEM((TS + M, depth), jnp.bfloat16),
            pltpu.VMEM((TS, LANES), jnp.float32),
            pltpu.VMEM((TS + M - JOIN * STEP, unit + M), jnp.float32),
            pltpu.VMEM((units, 8, unit + M), jnp.float32),
        ],
        compiler_params=pltpu.CompilerParams(vmem_limit_bytes=32 * 2**20),
    )(series, lists, own, norms)
    mine = pltpu.with_memory_space_constraint(mine, pltpu.VMEM)
    theirs = pl.pallas_call(
        swap_kernel,
        out_shape=pltpu.VMEM(shape, jnp.float32),
        in_specs=[inside],
        out_specs=inside,
        scratch_shapes=[pltpu.SemaphoreType.DMA((2,))],
        compiler_params=pltpu.CompilerParams(
            collective_id=1, has_side_effects=True, vmem_limit_bytes=16 * 2**20
        ),
    )(mine)
    theirs = pltpu.with_memory_space_constraint(theirs, pltpu.VMEM)
    out = pl.pallas_call(
        lower_kernel,
        out_shape=jax.ShapeDtypeStruct(shape, jnp.float32),
        in_specs=[inside] * 2,
        out_specs=inside,
        compiler_params=pltpu.CompilerParams(vmem_limit_bytes=16 * 2**20),
    )(mine, theirs)
    return out.reshape(-1)


def solution(mesh):
    placed = (P("ch", ("grp", "tm")), P(None, "grp"), P(), P(("grp", "tm"), "sub", None, None))
    return jax.shard_map(
        body, mesh=mesh, in_specs=placed, out_specs=P(("grp", "tm", "sub")), check_vma=False
    )
```

```python
import functools

import jax
import jax.numpy as jnp
from jax import lax
from jax.experimental import pallas as pl
from jax.experimental.pallas import tpu as pltpu
from jax.sharding import PartitionSpec as P

M = 128
TS = 512
SLOTS = 2
DEPTH = 2048
EXCL = 32
LANES = 128
STEP = 16
JOIN = 2
MESH = pl.DeviceIdType.MESH


def whiten(factor, samples):
    return jnp.dot(
        factor, samples, precision=lax.Precision.HIGHEST, preferred_element_type=jnp.float32
    ).astype(jnp.bfloat16)


def lag(series_ref, first_tile, count, scale):
    channels = series_ref.shape[1]
    pieces = [series_ref[first_tile + k].astype(jnp.float32) for k in range(count)]
    segment = jnp.concatenate(pieces, axis=1)
    width = count * LANES
    column = lax.broadcasted_iota(jnp.int32, (channels, LANES), 1)
    turned = {}

    def turn(k, l):
        k = min(k, count - 1)
        if (k, l) not in turned:
            turned[k, l] = pieces[k] if l == 0 else pltpu.roll(pieces[k], LANES - l, axis=1)
        return turned[k, l]

    def moved(k, l):
        here = turn(k, l)
        here = here if l == 0 else jnp.where(column < LANES - l, here, turn(k + 1, l))
        return here.astype(jnp.bfloat16)

    lagged = []
    for at in range(0, count, 2):
        tiles = range(at, min(at + 2, count))
        size = len(tiles) * LANES
        hankel = jnp.concatenate(
            [jnp.concatenate([moved(k, l) for k in tiles], axis=1) for l in range(STEP)], axis=0
        )
        unit_matrix = jnp.where(
            lax.broadcasted_iota(jnp.int32, (size, size), 0)
            == lax.broadcasted_iota(jnp.int32, (size, size), 1),
            scale,
            0.0,
        ).astype(jnp.bfloat16)
        lagged.append(
            lax.dot_general(
                unit_matrix, hankel, (((1,), (1,)), ((), ())), preferred_element_type=jnp.float32
            ).astype(jnp.bfloat16)
        )
    norms = jnp.broadcast_to(jnp.sum(segment * segment, axis=0, keepdims=True), (8, width))
    shift = 1
    while shift < M:
        norms = norms + pltpu.roll(norms, width - shift, axis=1)
        shift *= 2
    return lagged, norms


def own_columns(series_ref, own_tile, mine_ref, norms_ref):
    units, unit_cols, joined = mine_ref.shape
    depth = joined // JOIN
    n_tiles = unit_cols // LANES
    unit = unit_cols - M
    lagged, norms_ref[...] = lag(series_ref, own_tile, units * unit // LANES + 1, 1.0)
    groups = [piece[at : at + STEP] for piece in lagged for at in range(0, piece.shape[0], STEP)]
    for u in range(units):
        for q in range(unit_cols // STEP):
            place = ((q % n_tiles) * 8 + q // n_tiles) * STEP
            for v in range(JOIN):
                at = min(u * unit // STEP + q + v, len(groups) - 1)
                mine_ref[u, place : place + STEP, v * depth : (v + 1) * depth] = groups[at]


def gather_kernel(
    n_tm,
    n_sub,
    tiles_hbm,
    archive_hbm,
    tail_hbm,
    precision_hbm,
    series_ref,
    lists_smem,
    mine_ref,
    norms_ref,
    lists_ref,
    tail_ref,
    precision_ref,
    raw_ref,
    load_sems,
    raw_sems,
    time_send,
    time_recv,
    pair_send,
    pair_recv,
    list_send,
    list_recv,
    here_sems,
):
    tm, sub, ch = lax.axis_index("tm"), lax.axis_index("sub"), lax.axis_index("ch")
    other = 1 - ch
    owners = n_tm * n_sub
    me = tm * n_sub + sub
    channels, span = archive_hbm.shape
    half = span // 2
    tiles = half // LANES
    last = n_tm * span // LANES

    def send(source, target, sem, landed, device):
        return pltpu.make_async_remote_copy(
            src_ref=source,
            dst_ref=target,
            send_sem=sem,
            recv_sem=landed,
            device_id=device,
            device_id_type=MESH,
        )

    def each_owner(action):
        if owners <= 16:
            for rank in range(owners):
                action(rank, rank // n_sub, rank % n_sub)
        else:
            lax.fori_loop(
                0, owners, lambda rank, _: (action(rank, rank // n_sub, rank % n_sub), 0)[1], 0
            )

    def above(rank, t, s):
        return (t >= tm) & (s >= sub) & (rank != me)

    def below(rank, t, s):
        return (t <= tm) & (s <= sub) & (rank != me)

    barrier = pltpu.get_barrier_semaphore()
    pl.semaphore_signal(barrier, inc=1, device_id={"ch": other}, device_id_type=MESH)

    def announce(rank, t, s):
        @pl.when(above(rank, t, s))
        def _():
            pl.semaphore_signal(
                barrier, inc=1, device_id={"tm": t, "sub": s}, device_id_type=MESH
            )

    each_owner(announce)
    own_rows = pl.ds(pl.multiple_of(ch * channels, channels), channels)
    own_half = archive_hbm.at[:, pl.ds(pl.multiple_of(ch * half, half), half)]
    own_list = lists_ref.at[me]
    loads = [
        pltpu.make_async_copy(source, target, load_sems.at[at])
        for at, (source, target) in enumerate(
            (
                (precision_hbm, precision_ref),
                (tail_hbm, tail_ref),
                (own_half, raw_ref.at[own_rows, :]),
                (tiles_hbm.at[0, 0], own_list),
            )
        )
    ]
    for load in loads:
        load.start()
    pl.semaphore_wait(barrier, (tm + 1) * (sub + 1))

    swap = send(
        archive_hbm.at[:, pl.ds(pl.multiple_of(other * half, half), half)],
        raw_ref.at[own_rows, :],
        raw_sems.at[0],
        raw_sems.at[1],
        {"ch": other},
    )
    swap.start()

    def direct(rank, t, s):
        return send(
            tiles_hbm.at[0, 0],
            own_list,
            list_send.at[rank],
            list_recv.at[me],
            {"tm": t, "sub": s},
        )

    def answer(rank, t, s):
        @pl.when(below(rank, t, s))
        def _():
            pl.semaphore_signal(
                here_sems.at[me], inc=1, device_id={"tm": t, "sub": s}, device_id_type=MESH
            )
            direct(rank, t, s).start()

    each_owner(answer)
    for load in loads[:2]:
        load.wait()
    factor = precision_ref[...]
    series_ref[last] = jnp.zeros((2 * channels, LANES), jnp.bfloat16)
    series_ref[last, :, : M - 1] = whiten(factor, tail_ref[...])
    for load in loads[2:]:
        load.wait()
    swap.wait_recv()

    def chunk(owner, part):
        return series_ref.at[pl.ds((owner * 2 + part) * tiles, tiles)]

    mine = chunk(tm, ch)
    whitened = whiten(factor, raw_ref[...])
    for k in range(tiles):
        series_ref[(tm * 2 + ch) * tiles + k] = whitened[:, k * LANES : (k + 1) * LANES]

    def along_time(t):
        return send(mine, mine, time_send.at[t], time_recv.at[tm], {"tm": t})

    to_pair = []

    def forward(held):
        step = len(to_pair)
        copy = send(held, held, pair_send.at[step], pair_recv.at[step], {"ch": other})
        to_pair.append(copy)
        copy.start()

    for t in range(n_tm):
        pl.when(t < tm)(along_time(t).start)
    forward(mine)
    for t in range(1, n_tm):

        @pl.when(t > tm)
        def _():
            pl.semaphore_wait(here_sems.at[t * n_sub + sub], 1)
            along_time(t).start()
            for s in range(n_sub):
                pl.when(s <= sub)(direct(t * n_sub + s, t, s).start)

    def list_up(rank, t, s):
        @pl.when(above(rank, t, s) & (s != sub))
        def _():
            pl.semaphore_wait(here_sems.at[rank], 1)
            direct(rank, t, s).start()
            for back in range(n_tm):
                pl.when((t == tm) & (back < tm))(direct(back * n_sub + s, back, s).start)

    each_owner(list_up)

    def landed(rank):
        held = lists_ref.at[rank]
        return send(held, held, list_send.at[0], list_recv.at[rank], {"ch": other})

    own_tile = me * (span // n_sub // LANES)
    early = (sub != n_sub - 1) | (tm == 0) | (tm == n_tm - 1)

    def prepare():
        own_columns(series_ref, own_tile, mine_ref, norms_ref)

    for step in range(1, n_tm):
        source = step + ((tm + n_tm - step) // n_tm) * (tm - 2 * step)
        held = chunk(source, ch)
        send(held, held, time_send.at[0], time_recv.at[source], {"ch": other}).wait_recv()
        forward(held)
        if step == 1:
            for copy in to_pair:
                copy.wait_recv()
            pl.when(early)(prepare)
    each_owner(lambda rank, t, s: pl.when(rank != me)(landed(rank).wait_recv))
    keep = pltpu.make_async_copy(lists_ref, lists_smem, load_sems.at[0])
    keep.start()
    for copy in to_pair[2:]:
        copy.wait_recv()
    pl.when(jnp.logical_not(early))(prepare)
    keep.wait()

    swap.wait_send()
    for copy in to_pair:
        copy.wait_send()
    for t in range(n_tm):
        pl.when(t != tm)(along_time(t).wait_send)
    each_owner(lambda rank, t, s: pl.when(rank != me)(direct(rank, t, s).wait_send))


def match_kernel(
    n_sub,
    series_ref,
    lists_smem,
    mine_ref,
    norms_ref,
    out_ref,
    work_smem,
    lagged_ref,
    wide_ref,
    products_ref,
    best_ref,
):
    units, unit_cols, _ = mine_ref.shape
    n_tiles = unit_cols // LANES
    unit = unit_cols - M
    per_block = TS // LANES
    rows = TS + M
    ch = lax.axis_index("ch")
    me = lax.axis_index("tm") * n_sub + lax.axis_index("sub")
    own_tile = me * (units * unit // LANES)
    for u in range(units):
        best_ref[u] = jnp.full((8, unit_cols), jnp.inf, jnp.float32)
    lane = lax.broadcasted_iota(jnp.int32, (8, LANES), 1)
    own_at = [((lane // STEP) * n_tiles + t) * STEP + lane % STEP for t in range(n_tiles)]
    sublane = lax.broadcasted_iota(jnp.int32, (8, LANES), 0)

    owners = lists_smem.shape[0]

    def scan(owner, found):
        for slot in range(SLOTS):
            row_block, col_block = lists_smem[owner, slot, 0], lists_smem[owner, slot, 1]
            for u in range(units):
                block = (own_tile * LANES + u * unit) // TS
                work_smem[found] = (row_block + col_block - block) * units + u
                hit = (row_block == block) | (col_block == block)
                found = found + hit.astype(jnp.int32)
        return found

    if owners <= 16:
        found = jnp.int32(0)
        for owner in range(owners):
            found = scan(owner, found)
    else:
        found = lax.fori_loop(0, owners, scan, jnp.int32(0))

    def ahead(tiles, at):
        turn = at // n_tiles
        tile = tiles[at % n_tiles]
        return tile if turn == 0 else pltpu.roll(tile, LANES - turn * STEP, axis=1)

    def keep_apart(offset):
        for g in range(products_ref.shape[0] // STEP):
            if g % (M // STEP) < JOIN:
                for at in range(g * STEP, (g + 1) * STEP, 8):
                    for t in range(n_tiles):
                        here = (pl.ds(at, 8), pl.ds(t * LANES, LANES))
                        apart = (sublane + (at + offset)) - own_at[t]
                        products_ref[here] = jnp.where(
                            jnp.abs(apart) < EXCL, jnp.inf, products_ref[here]
                        )

    def reduce(u):
        low = [best_ref[u, :, t * LANES : (t + 1) * LANES] for t in range(n_tiles)]
        for part in range(0, STEP, 8):
            sums = {}
            for g in range(products_ref.shape[0] // STEP):
                at = g * STEP + part
                sums[JOIN, g] = [
                    products_ref[at : at + 8, t * LANES : (t + 1) * LANES] for t in range(n_tiles)
                ]
                first, size = g, JOIN
                while size < M // STEP and first >= size:
                    first -= size
                    early, late = sums[size, first], sums[size, first + size]
                    sums[2 * size, first] = [
                        early[t] + ahead(late, t + size) for t in range(n_tiles)
                    ]
                    size *= 2
                if size == M // STEP:
                    at = first * STEP + part
                    wide = wide_ref[at : at + 8, :]
                    for t in range(n_tiles):
                        low[t] = jnp.minimum(low[t], sums[size, first][t] + wide)
        for t in range(n_tiles):
            best_ref[u, :, t * LANES : (t + 1) * LANES] = low[t]

    def incidence(at, _):
        entry = work_smem[2 * at + ch]
        u = entry % units
        partner = entry // units
        lagged, norms = lag(series_ref, partner * per_block, rows // LANES, -2.0)
        place = 0
        for piece in lagged:
            lagged_ref[place : place + piece.shape[0], :] = piece
            place += piece.shape[0]
        for k in range(per_block):
            one = jnp.broadcast_to(norms[:1, k * LANES : (k + 1) * LANES], (LANES, LANES))
            wide_ref[k * LANES : (k + 1) * LANES, :] = jnp.transpose(one)
        longer = [lagged_ref[v * STEP : v * STEP + products_ref.shape[0], :] for v in range(JOIN)]
        products_ref[...] = lax.dot_general(
            jnp.concatenate(longer, axis=1) if JOIN > 1 else longer[0],
            mine_ref[u],
            (((1,), (1,)), ((), ())),
            preferred_element_type=jnp.float32,
        )
        offset = partner * TS - (own_tile * LANES + u * unit)
        keep_apart(offset)
        reduce(u)
        return 0

    lax.fori_loop(0, (found + 1 - ch) // 2, incidence, 0)

    group = lane // STEP
    for u in range(units):
        low = jnp.min(best_ref[u], axis=0, keepdims=True)
        tiles = [
            jnp.broadcast_to(low[:, t * LANES : (t + 1) * LANES], (8, LANES)) for t in range(n_tiles)
        ]
        for k in range(unit // LANES):
            natural = None
            for g in range(LANES // STEP):
                q = k * (LANES // STEP) + g
                turn = (g - q // n_tiles) % (LANES // STEP)
                tile = tiles[q % n_tiles]
                tile = tile if turn == 0 else pltpu.roll(tile, turn * STEP, axis=1)
                natural = tile if natural is None else jnp.where(group == g, tile, natural)
            at = u * (unit // LANES) + k
            done = (natural[:1] + norms_ref[:1, at * LANES : (at + 1) * LANES]) * (1.0 / DEPTH)
            out_ref[at : at + 1, :] = done


def swap_kernel(mine_ref, theirs_ref, sems):
    other = {"ch": 1 - lax.axis_index("ch")}
    barrier = pltpu.get_barrier_semaphore()
    pl.semaphore_signal(barrier, inc=1, device_id=other, device_id_type=MESH)
    pl.semaphore_wait(barrier, 1)
    copy = pltpu.make_async_remote_copy(
        src_ref=mine_ref,
        dst_ref=theirs_ref,
        send_sem=sems.at[0],
        recv_sem=sems.at[1],
        device_id=other,
        device_id_type=MESH,
    )
    copy.start()
    copy.wait()


def lower_kernel(mine_ref, theirs_ref, out_ref):
    out_ref[...] = jnp.minimum(mine_ref[...], theirs_ref[...])


def body(archive, tail, precision, tile_list):
    n_tm, n_sub = lax.axis_size("tm"), lax.axis_size("sub")
    owners = n_tm * n_sub
    channels, span = archive.shape
    piece = span // n_sub
    unit = min(piece, TS)
    units = piece // unit
    every = 2 * channels
    depth = STEP * every
    anywhere = pl.BlockSpec(memory_space=pltpu.HBM)
    inside = pl.BlockSpec(memory_space=pltpu.VMEM)
    scalars = pl.BlockSpec(memory_space=pltpu.SMEM)
    series, lists, own, norms = pl.pallas_call(
        functools.partial(gather_kernel, n_tm, n_sub),
        out_shape=[
            pltpu.VMEM((n_tm * span // LANES + 1, every, LANES), jnp.bfloat16),
            pltpu.SMEM((owners,) + tile_list.shape[2:], jnp.int32),
            pltpu.VMEM((units, unit + M, JOIN * depth), jnp.bfloat16),
            pltpu.VMEM((8, piece + M), jnp.float32),
        ],
        in_specs=[anywhere] * 4,
        out_specs=[inside, scalars, inside, inside],
        scratch_shapes=[
            pltpu.VMEM((owners,) + tile_list.shape[2:], jnp.int32),
            pltpu.VMEM(tail.shape, jnp.float32),
            pltpu.VMEM(precision.shape, jnp.float32),
            pltpu.VMEM((every, span // 2), jnp.float32),
            pltpu.SemaphoreType.DMA((4,)),
            pltpu.SemaphoreType.DMA((2,)),
            pltpu.SemaphoreType.DMA((n_tm,)),
            pltpu.SemaphoreType.DMA((n_tm,)),
            pltpu.SemaphoreType.DMA((n_tm,)),
            pltpu.SemaphoreType.DMA((n_tm,)),
            pltpu.SemaphoreType.DMA((owners,)),
            pltpu.SemaphoreType.DMA((owners,)),
            pltpu.SemaphoreType.REGULAR((owners,)),
        ],
        compiler_params=pltpu.CompilerParams(
            collective_id=0, has_side_effects=True, vmem_limit_bytes=62 * 2**20
        ),
    )(tile_list, archive, tail, precision)
    series, own, norms = [
        pltpu.with_memory_space_constraint(array, pltpu.VMEM) for array in (series, own, norms)
    ]
    lists = pltpu.with_memory_space_constraint(lists, pltpu.SMEM)
    shape = (piece // LANES, LANES)
    mine = pl.pallas_call(
        functools.partial(match_kernel, n_sub),
        out_shape=pltpu.VMEM(shape, jnp.float32),
        in_specs=[inside, scalars, inside, inside],
        out_specs=inside,
        scratch_shapes=[
            pltpu.SMEM((owners * SLOTS * units + 1,), jnp.int32),
            pltpu.VMEM((TS + M, depth), jnp.bfloat16),
            pltpu.VMEM((TS, LANES), jnp.float32),
            pltpu.VMEM((TS + M - JOIN * STEP, unit + M), jnp.float32),
            pltpu.VMEM((units, 8, unit + M), jnp.float32),
        ],
        compiler_params=pltpu.CompilerParams(vmem_limit_bytes=32 * 2**20),
    )(series, lists, own, norms)
    mine = pltpu.with_memory_space_constraint(mine, pltpu.VMEM)
    theirs = pl.pallas_call(
        swap_kernel,
        out_shape=pltpu.VMEM(shape, jnp.float32),
        in_specs=[inside],
        out_specs=inside,
        scratch_shapes=[pltpu.SemaphoreType.DMA((2,))],
        compiler_params=pltpu.CompilerParams(
            collective_id=1, has_side_effects=True, vmem_limit_bytes=16 * 2**20
        ),
    )(mine)
    theirs = pltpu.with_memory_space_constraint(theirs, pltpu.VMEM)
    out = pl.pallas_call(
        lower_kernel,
        out_shape=jax.ShapeDtypeStruct(shape, jnp.float32),
        in_specs=[inside] * 2,
        out_specs=inside,
        compiler_params=pltpu.CompilerParams(vmem_limit_bytes=16 * 2**20),
    )(mine, theirs)
    return out.reshape(-1)


def solution(mesh):
    placed = (P("ch", ("grp", "tm")), P(None, "grp"), P(), P(("grp", "tm"), "sub", None, None))
    return jax.shard_map(
        body, mesh=mesh, in_specs=placed, out_specs=P(("grp", "tm", "sub")), check_vma=False
    )
```

```python
import functools

import jax
import jax.numpy as jnp
from jax import lax
from jax.experimental import pallas as pl
from jax.experimental.pallas import tpu as pltpu
from jax.sharding import PartitionSpec as P

M = 128
TS = 512
SLOTS = 2
DEPTH = 2048
EXCL = 32
LANES = 128
STEP = 16
JOIN = 2
MESH = pl.DeviceIdType.MESH


def whiten(factor, samples):
    return jnp.dot(
        factor, samples, precision=lax.Precision.HIGHEST, preferred_element_type=jnp.float32
    ).astype(jnp.bfloat16)


def lag(series_ref, first_tile, count, scale):
    channels = series_ref.shape[1]
    pieces = [series_ref[first_tile + k].astype(jnp.float32) for k in range(count)]
    segment = jnp.concatenate(pieces, axis=1)
    width = count * LANES
    column = lax.broadcasted_iota(jnp.int32, (channels, LANES), 1)
    turned = {}

    def turn(k, l):
        k = min(k, count - 1)
        if (k, l) not in turned:
            turned[k, l] = pieces[k] if l == 0 else pltpu.roll(pieces[k], LANES - l, axis=1)
        return turned[k, l]

    def moved(k, l):
        here = turn(k, l)
        here = here if l == 0 else jnp.where(column < LANES - l, here, turn(k + 1, l))
        return here.astype(jnp.bfloat16)

    near = []
    for at in range(0, count, 2):
        tiles = range(at, min(at + 2, count))
        hankel = jnp.concatenate(
            [jnp.concatenate([moved(k, l) for k in tiles], axis=1) for l in range(8)], axis=0
        )
        size = len(tiles) * LANES
        unit_matrix = jnp.where(
            lax.broadcasted_iota(jnp.int32, (size, size), 0)
            == lax.broadcasted_iota(jnp.int32, (size, size), 1),
            scale,
            0.0,
        ).astype(jnp.bfloat16)
        near.append(
            lax.dot_general(
                unit_matrix, hankel, (((1,), (1,)), ((), ())), preferred_element_type=jnp.float32
            )
        )
    lagged = []
    for at, piece in enumerate(near):
        after = near[min(at + 1, len(near) - 1)]
        late = jnp.concatenate([piece[8:], after[:8]], axis=0)
        lagged.append(
            jnp.concatenate([piece.astype(jnp.bfloat16), late.astype(jnp.bfloat16)], axis=1)
        )
    norms = jnp.broadcast_to(jnp.sum(segment * segment, axis=0, keepdims=True), (8, width))
    shift = 1
    while shift < M:
        norms = norms + pltpu.roll(norms, width - shift, axis=1)
        shift *= 2
    return lagged, norms


def own_columns(series_ref, own_tile, mine_ref, norms_ref):
    units, unit_cols, joined = mine_ref.shape
    depth = joined // JOIN
    n_tiles = unit_cols // LANES
    unit = unit_cols - M
    lagged, norms_ref[...] = lag(series_ref, own_tile, units * unit // LANES + 1, 1.0)
    groups = [piece[at : at + STEP] for piece in lagged for at in range(0, piece.shape[0], STEP)]
    for u in range(units):
        for q in range(unit_cols // STEP):
            place = ((q % n_tiles) * 8 + q // n_tiles) * STEP
            for v in range(JOIN):
                at = min(u * unit // STEP + q + v, len(groups) - 1)
                mine_ref[u, place : place + STEP, v * depth : (v + 1) * depth] = groups[at]


def gather_kernel(
    n_tm,
    n_sub,
    tiles_hbm,
    archive_hbm,
    tail_hbm,
    precision_hbm,
    series_ref,
    lists_smem,
    mine_ref,
    norms_ref,
    lists_ref,
    tail_ref,
    precision_ref,
    raw_ref,
    load_sems,
    raw_sems,
    time_send,
    time_recv,
    pair_send,
    pair_recv,
    list_send,
    list_recv,
    here_sems,
):
    tm, sub, ch = lax.axis_index("tm"), lax.axis_index("sub"), lax.axis_index("ch")
    other = 1 - ch
    owners = n_tm * n_sub
    me = tm * n_sub + sub
    channels, span = archive_hbm.shape
    half = span // 2
    tiles = half // LANES
    last = n_tm * span // LANES

    def send(source, target, sem, landed, device):
        return pltpu.make_async_remote_copy(
            src_ref=source,
            dst_ref=target,
            send_sem=sem,
            recv_sem=landed,
            device_id=device,
            device_id_type=MESH,
        )

    def each_owner(action):
        if owners <= 16:
            for rank in range(owners):
                action(rank, rank // n_sub, rank % n_sub)
        else:
            lax.fori_loop(
                0, owners, lambda rank, _: (action(rank, rank // n_sub, rank % n_sub), 0)[1], 0
            )

    def above(rank, t, s):
        return (t >= tm) & (s >= sub) & (rank != me)

    def below(rank, t, s):
        return (t <= tm) & (s <= sub) & (rank != me)

    barrier = pltpu.get_barrier_semaphore()
    pl.semaphore_signal(barrier, inc=1, device_id={"ch": other}, device_id_type=MESH)

    def announce(rank, t, s):
        @pl.when(above(rank, t, s))
        def _():
            pl.semaphore_signal(
                barrier, inc=1, device_id={"tm": t, "sub": s}, device_id_type=MESH
            )

    own_rows = pl.ds(pl.multiple_of(ch * channels, channels), channels)
    own_half = archive_hbm.at[:, pl.ds(pl.multiple_of(ch * half, half), half)]
    own_list = lists_ref.at[me]
    loads = [
        pltpu.make_async_copy(source, target, load_sems.at[at])
        for at, (source, target) in enumerate(
            (
                (precision_hbm, precision_ref),
                (tail_hbm, tail_ref),
                (own_half, raw_ref.at[own_rows, :]),
                (tiles_hbm.at[0, 0], own_list),
            )
        )
    ]
    for load in loads:
        load.start()
    each_owner(announce)
    pl.semaphore_wait(barrier, (tm + 1) * (sub + 1))

    swap = send(
        archive_hbm.at[:, pl.ds(pl.multiple_of(other * half, half), half)],
        raw_ref.at[own_rows, :],
        raw_sems.at[0],
        raw_sems.at[1],
        {"ch": other},
    )
    swap.start()

    def direct(rank, t, s):
        return send(
            tiles_hbm.at[0, 0],
            own_list,
            list_send.at[rank],
            list_recv.at[me],
            {"tm": t, "sub": s},
        )

    def answer(rank, t, s):
        @pl.when(below(rank, t, s))
        def _():
            pl.semaphore_signal(
                here_sems.at[me], inc=1, device_id={"tm": t, "sub": s}, device_id_type=MESH
            )
            direct(rank, t, s).start()

    each_owner(answer)
    for load in loads[:2]:
        load.wait()
    factor = precision_ref[...]
    series_ref[last] = jnp.zeros((2 * channels, LANES), jnp.bfloat16)
    series_ref[last, :, : M - 1] = whiten(factor, tail_ref[...])
    for load in loads[2:]:
        load.wait()
    swap.wait_recv()

    def chunk(owner, part):
        return series_ref.at[pl.ds((owner * 2 + part) * tiles, tiles)]

    mine = chunk(tm, ch)
    whitened = whiten(factor, raw_ref[...])
    for k in range(tiles):
        series_ref[(tm * 2 + ch) * tiles + k] = whitened[:, k * LANES : (k + 1) * LANES]

    def along_time(t):
        return send(mine, mine, time_send.at[t], time_recv.at[tm], {"tm": t})

    to_pair = []

    def forward(held):
        step = len(to_pair)
        copy = send(held, held, pair_send.at[step], pair_recv.at[step], {"ch": other})
        to_pair.append(copy)
        copy.start()

    for t in range(n_tm):
        pl.when(t < tm)(along_time(t).start)
    forward(mine)
    for t in range(1, n_tm):

        @pl.when(t > tm)
        def _():
            pl.semaphore_wait(here_sems.at[t * n_sub + sub], 1)
            along_time(t).start()
            for s in range(n_sub):
                pl.when(s <= sub)(direct(t * n_sub + s, t, s).start)

    def list_up(rank, t, s):
        @pl.when(above(rank, t, s) & (s != sub))
        def _():
            pl.semaphore_wait(here_sems.at[rank], 1)
            direct(rank, t, s).start()
            for back in range(n_tm):
                pl.when((t == tm) & (back < tm))(direct(back * n_sub + s, back, s).start)

    each_owner(list_up)

    def landed(rank):
        held = lists_ref.at[rank]
        return send(held, held, list_send.at[0], list_recv.at[rank], {"ch": other})

    own_tile = me * (span // n_sub // LANES)
    early = (sub != n_sub - 1) | (tm == 0) | (tm == n_tm - 1)

    def prepare():
        own_columns(series_ref, own_tile, mine_ref, norms_ref)

    for step in range(1, n_tm):
        source = step + ((tm + n_tm - step) // n_tm) * (tm - 2 * step)
        held = chunk(source, ch)
        send(held, held, time_send.at[0], time_recv.at[source], {"ch": other}).wait_recv()
        forward(held)
        if step == 1:
            for copy in to_pair:
                copy.wait_recv()
            pl.when(early)(prepare)
    each_owner(lambda rank, t, s: pl.when(rank != me)(landed(rank).wait_recv))
    keep = pltpu.make_async_copy(lists_ref, lists_smem, load_sems.at[0])
    keep.start()
    swap.wait_send()
    for t in range(n_tm):
        pl.when(t != tm)(along_time(t).wait_send)
    each_owner(lambda rank, t, s: pl.when(rank != me)(direct(rank, t, s).wait_send))
    for copy in to_pair:
        copy.wait_send()
    for copy in to_pair[2:]:
        copy.wait_recv()
    pl.when(jnp.logical_not(early))(prepare)
    keep.wait()


def match_kernel(
    n_sub,
    series_ref,
    lists_smem,
    mine_ref,
    norms_ref,
    out_ref,
    work_smem,
    lagged_ref,
    wide_ref,
    products_ref,
    best_ref,
):
    units, unit_cols, _ = mine_ref.shape
    n_tiles = unit_cols // LANES
    unit = unit_cols - M
    per_block = TS // LANES
    rows = TS + M
    tm, ch = lax.axis_index("tm"), lax.axis_index("ch")
    me = tm * n_sub + lax.axis_index("sub")
    share = jnp.where(tm == 0, 1 - ch, ch)
    own_tile = me * (units * unit // LANES)
    for u in range(units):
        best_ref[u] = jnp.full((8, unit_cols), jnp.inf, jnp.float32)
    lane = lax.broadcasted_iota(jnp.int32, (8, LANES), 1)
    own_at = [((lane // STEP) * n_tiles + t) * STEP + lane % STEP for t in range(n_tiles)]
    sublane = lax.broadcasted_iota(jnp.int32, (8, LANES), 0)

    owners = lists_smem.shape[0]

    def scan(owner, found):
        for slot in range(SLOTS):
            row_block, col_block = lists_smem[owner, slot, 0], lists_smem[owner, slot, 1]
            for u in range(units):
                block = (own_tile * LANES + u * unit) // TS
                work_smem[found] = (row_block + col_block - block) * units + u
                hit = (row_block == block) | (col_block == block)
                found = found + hit.astype(jnp.int32)
        return found

    if owners <= 16:
        found = jnp.int32(0)
        for owner in range(owners):
            found = scan(owner, found)
    else:
        found = lax.fori_loop(0, owners, scan, jnp.int32(0))

    def ahead(tiles, at):
        turn = at // n_tiles
        tile = tiles[at % n_tiles]
        return tile if turn == 0 else pltpu.roll(tile, LANES - turn * STEP, axis=1)

    def keep_apart(offset):
        for g in range(products_ref.shape[0] // STEP):
            if g % (M // STEP) < JOIN:
                for at in range(g * STEP, (g + 1) * STEP, 8):
                    for t in range(n_tiles):
                        here = (pl.ds(at, 8), pl.ds(t * LANES, LANES))
                        apart = (sublane + (at + offset)) - own_at[t]
                        products_ref[here] = jnp.where(
                            jnp.abs(apart) < EXCL, jnp.inf, products_ref[here]
                        )

    def reduce(u):
        low = [best_ref[u, :, t * LANES : (t + 1) * LANES] for t in range(n_tiles)]
        for part in range(0, STEP, 8):
            sums = {}
            for g in range(products_ref.shape[0] // STEP):
                at = g * STEP + part
                sums[JOIN, g] = [
                    products_ref[at : at + 8, t * LANES : (t + 1) * LANES] for t in range(n_tiles)
                ]
                first, size = g, JOIN
                while size < M // STEP and first >= size:
                    first -= size
                    early, late = sums[size, first], sums[size, first + size]
                    sums[2 * size, first] = [
                        early[t] + ahead(late, t + size) for t in range(n_tiles)
                    ]
                    size *= 2
                if size == M // STEP:
                    at = first * STEP + part
                    wide = wide_ref[at : at + 8, :]
                    for t in range(n_tiles):
                        low[t] = jnp.minimum(low[t], sums[size, first][t] + wide)
        for t in range(n_tiles):
            best_ref[u, :, t * LANES : (t + 1) * LANES] = low[t]

    def incidence(at, _):
        entry = work_smem[2 * at + share]
        u = entry % units
        partner = entry // units
        lagged, norms = lag(series_ref, partner * per_block, rows // LANES, -2.0)
        place = 0
        for piece in lagged:
            lagged_ref[place : place + piece.shape[0], :] = piece
            place += piece.shape[0]
        for k in range(per_block):
            one = jnp.broadcast_to(norms[:1, k * LANES : (k + 1) * LANES], (LANES, LANES))
            wide_ref[k * LANES : (k + 1) * LANES, :] = jnp.transpose(one)
        longer = [lagged_ref[v * STEP : v * STEP + products_ref.shape[0], :] for v in range(JOIN)]
        products_ref[...] = lax.dot_general(
            jnp.concatenate(longer, axis=1) if JOIN > 1 else longer[0],
            mine_ref[u],
            (((1,), (1,)), ((), ())),
            preferred_element_type=jnp.float32,
        )
        offset = partner * TS - (own_tile * LANES + u * unit)
        keep_apart(offset)
        reduce(u)
        return 0

    lax.fori_loop(0, (found + 1 - share) // 2, incidence, 0)

    group = lane // STEP
    for u in range(units):
        low = jnp.min(best_ref[u], axis=0, keepdims=True)
        tiles = [
            jnp.broadcast_to(low[:, t * LANES : (t + 1) * LANES], (8, LANES)) for t in range(n_tiles)
        ]
        for k in range(unit // LANES):
            natural = None
            for g in range(LANES // STEP):
                q = k * (LANES // STEP) + g
                turn = (g - q // n_tiles) % (LANES // STEP)
                tile = tiles[q % n_tiles]
                tile = tile if turn == 0 else pltpu.roll(tile, turn * STEP, axis=1)
                natural = tile if natural is None else jnp.where(group == g, tile, natural)
            at = u * (unit // LANES) + k
            done = (natural[:1] + norms_ref[:1, at * LANES : (at + 1) * LANES]) * (1.0 / DEPTH)
            out_ref[at : at + 1, :] = done


def swap_kernel(mine_ref, theirs_ref, sems):
    other = {"ch": 1 - lax.axis_index("ch")}
    barrier = pltpu.get_barrier_semaphore()
    pl.semaphore_signal(barrier, inc=1, device_id=other, device_id_type=MESH)
    pl.semaphore_wait(barrier, 1)
    copy = pltpu.make_async_remote_copy(
        src_ref=mine_ref,
        dst_ref=theirs_ref,
        send_sem=sems.at[0],
        recv_sem=sems.at[1],
        device_id=other,
        device_id_type=MESH,
    )
    copy.start()
    copy.wait()


def lower_kernel(mine_ref, theirs_ref, out_ref):
    out_ref[...] = jnp.minimum(mine_ref[...], theirs_ref[...])


def body(archive, tail, precision, tile_list):
    n_tm, n_sub = lax.axis_size("tm"), lax.axis_size("sub")
    owners = n_tm * n_sub
    channels, span = archive.shape
    piece = span // n_sub
    unit = min(piece, TS)
    units = piece // unit
    every = 2 * channels
    depth = STEP * every
    anywhere = pl.BlockSpec(memory_space=pltpu.HBM)
    inside = pl.BlockSpec(memory_space=pltpu.VMEM)
    scalars = pl.BlockSpec(memory_space=pltpu.SMEM)
    series, lists, own, norms = pl.pallas_call(
        functools.partial(gather_kernel, n_tm, n_sub),
        out_shape=[
            pltpu.VMEM((n_tm * span // LANES + 1, every, LANES), jnp.bfloat16),
            pltpu.SMEM((owners,) + tile_list.shape[2:], jnp.int32),
            pltpu.VMEM((units, unit + M, JOIN * depth), jnp.bfloat16),
            pltpu.VMEM((8, piece + M), jnp.float32),
        ],
        in_specs=[anywhere] * 4,
        out_specs=[inside, scalars, inside, inside],
        scratch_shapes=[
            pltpu.VMEM((owners,) + tile_list.shape[2:], jnp.int32),
            pltpu.VMEM(tail.shape, jnp.float32),
            pltpu.VMEM(precision.shape, jnp.float32),
            pltpu.VMEM((every, span // 2), jnp.float32),
            pltpu.SemaphoreType.DMA((4,)),
            pltpu.SemaphoreType.DMA((2,)),
            pltpu.SemaphoreType.DMA((n_tm,)),
            pltpu.SemaphoreType.DMA((n_tm,)),
            pltpu.SemaphoreType.DMA((n_tm,)),
            pltpu.SemaphoreType.DMA((n_tm,)),
            pltpu.SemaphoreType.DMA((owners,)),
            pltpu.SemaphoreType.DMA((owners,)),
            pltpu.SemaphoreType.REGULAR((owners,)),
        ],
        compiler_params=pltpu.CompilerParams(
            collective_id=0, has_side_effects=True, vmem_limit_bytes=62 * 2**20
        ),
    )(tile_list, archive, tail, precision)
    series, own, norms = [
        pltpu.with_memory_space_constraint(array, pltpu.VMEM) for array in (series, own, norms)
    ]
    lists = pltpu.with_memory_space_constraint(lists, pltpu.SMEM)
    shape = (piece // LANES, LANES)
    mine = pl.pallas_call(
        functools.partial(match_kernel, n_sub),
        out_shape=pltpu.VMEM(shape, jnp.float32),
        in_specs=[inside, scalars, inside, inside],
        out_specs=inside,
        scratch_shapes=[
            pltpu.SMEM((owners * SLOTS * units + 1,), jnp.int32),
            pltpu.VMEM((TS + M, depth), jnp.bfloat16),
            pltpu.VMEM((TS, LANES), jnp.float32),
            pltpu.VMEM((TS + M - JOIN * STEP, unit + M), jnp.float32),
            pltpu.VMEM((units, 8, unit + M), jnp.float32),
        ],
        compiler_params=pltpu.CompilerParams(vmem_limit_bytes=32 * 2**20),
    )(series, lists, own, norms)
    mine = pltpu.with_memory_space_constraint(mine, pltpu.VMEM)
    theirs = pl.pallas_call(
        swap_kernel,
        out_shape=pltpu.VMEM(shape, jnp.float32),
        in_specs=[inside],
        out_specs=inside,
        scratch_shapes=[pltpu.SemaphoreType.DMA((2,))],
        compiler_params=pltpu.CompilerParams(
            collective_id=1, has_side_effects=True, vmem_limit_bytes=16 * 2**20
        ),
    )(mine)
    theirs = pltpu.with_memory_space_constraint(theirs, pltpu.VMEM)
    out = pl.pallas_call(
        lower_kernel,
        out_shape=jax.ShapeDtypeStruct(shape, jnp.float32),
        in_specs=[inside] * 2,
        out_specs=inside,
        compiler_params=pltpu.CompilerParams(vmem_limit_bytes=16 * 2**20),
    )(mine, theirs)
    return out.reshape(-1)


def solution(mesh):
    placed = (P("ch", ("grp", "tm")), P(None, "grp"), P(), P(("grp", "tm"), "sub", None, None))
    return jax.shard_map(
        body, mesh=mesh, in_specs=placed, out_specs=P(("grp", "tm", "sub")), check_vma=False
    )
```

```python
import functools

import jax
import jax.numpy as jnp
from jax import lax
from jax.experimental import pallas as pl
from jax.experimental.pallas import tpu as pltpu
from jax.sharding import PartitionSpec as P

M = 128
TS = 512
SLOTS = 2
DEPTH = 2048
EXCL = 32
LANES = 128
STEP = 16
JOIN = 2
PAIRED = 2
MESH = pl.DeviceIdType.MESH


def whiten(factor, samples):
    return jnp.dot(
        factor, samples, precision=lax.Precision.HIGHEST, preferred_element_type=jnp.float32
    ).astype(jnp.bfloat16)


def lag(series_ref, first_tile, count, scale):
    channels = series_ref.shape[1]
    pieces = [series_ref[first_tile + k].astype(jnp.float32) for k in range(count)]
    segment = jnp.concatenate(pieces, axis=1)
    width = count * LANES
    column = lax.broadcasted_iota(jnp.int32, (channels, LANES), 1)
    turned = {}

    def turn(k, l):
        k = min(k, count - 1)
        if (k, l) not in turned:
            turned[k, l] = pieces[k] if l == 0 else pltpu.roll(pieces[k], LANES - l, axis=1)
        return turned[k, l]

    def moved(k, l):
        here = turn(k, l)
        here = here if l == 0 else jnp.where(column < LANES - l, here, turn(k + 1, l))
        return here.astype(jnp.bfloat16)

    near = []
    for at in range(0, count, 2):
        tiles = range(at, min(at + 2, count))
        hankel = jnp.concatenate(
            [jnp.concatenate([moved(k, l) for k in tiles], axis=1) for l in range(8)], axis=0
        )
        size = len(tiles) * LANES
        unit_matrix = jnp.where(
            lax.broadcasted_iota(jnp.int32, (size, size), 0)
            == lax.broadcasted_iota(jnp.int32, (size, size), 1),
            scale,
            0.0,
        ).astype(jnp.bfloat16)
        near.append(
            lax.dot_general(
                unit_matrix, hankel, (((1,), (1,)), ((), ())), preferred_element_type=jnp.float32
            )
        )
    lagged = []
    for at, piece in enumerate(near):
        after = near[min(at + 1, len(near) - 1)]
        late = jnp.concatenate([piece[8:], after[:8]], axis=0)
        lagged.append(
            jnp.concatenate([piece.astype(jnp.bfloat16), late.astype(jnp.bfloat16)], axis=1)
        )
    norms = jnp.broadcast_to(jnp.sum(segment * segment, axis=0, keepdims=True), (8, width))
    shift = 1
    while shift < M:
        norms = norms + pltpu.roll(norms, width - shift, axis=1)
        shift *= 2
    return lagged, norms


def own_columns(series_ref, own_tile, mine_ref, norms_ref):
    units, unit_cols, joined = mine_ref.shape
    depth = joined // JOIN
    n_tiles = unit_cols // LANES
    unit = unit_cols - M
    lagged, norms_ref[...] = lag(series_ref, own_tile, units * unit // LANES + 1, 1.0)
    groups = [piece[at : at + STEP] for piece in lagged for at in range(0, piece.shape[0], STEP)]
    for u in range(units):
        for q in range(unit_cols // STEP):
            place = ((q % n_tiles) * 8 + q // n_tiles) * STEP
            for v in range(JOIN):
                at = min(u * unit // STEP + q + v, len(groups) - 1)
                mine_ref[u, place : place + STEP, v * depth : (v + 1) * depth] = groups[at]


def gather_kernel(
    n_tm,
    n_sub,
    tiles_hbm,
    archive_hbm,
    tail_hbm,
    precision_hbm,
    series_ref,
    lists_smem,
    mine_ref,
    norms_ref,
    lists_ref,
    tail_ref,
    precision_ref,
    raw_ref,
    load_sems,
    raw_sems,
    time_send,
    time_recv,
    pair_send,
    pair_recv,
    list_send,
    list_recv,
    here_sems,
):
    tm, sub, ch = lax.axis_index("tm"), lax.axis_index("sub"), lax.axis_index("ch")
    other = 1 - ch
    owners = n_tm * n_sub
    me = tm * n_sub + sub
    channels, span = archive_hbm.shape
    half = span // 2
    tiles = half // LANES
    last = n_tm * span // LANES

    def send(source, target, sem, landed, device):
        return pltpu.make_async_remote_copy(
            src_ref=source,
            dst_ref=target,
            send_sem=sem,
            recv_sem=landed,
            device_id=device,
            device_id_type=MESH,
        )

    def each_owner(action):
        if owners <= 16:
            for rank in range(owners):
                action(rank, rank // n_sub, rank % n_sub)
        else:
            lax.fori_loop(
                0, owners, lambda rank, _: (action(rank, rank // n_sub, rank % n_sub), 0)[1], 0
            )

    def above(rank, t, s):
        return (t >= tm) & (s >= sub) & (rank != me)

    def below(rank, t, s):
        return (t <= tm) & (s <= sub) & (rank != me)

    barrier = pltpu.get_barrier_semaphore()
    pl.semaphore_signal(barrier, inc=1, device_id={"ch": other}, device_id_type=MESH)

    def announce(rank, t, s):
        @pl.when(above(rank, t, s))
        def _():
            pl.semaphore_signal(
                barrier, inc=1, device_id={"tm": t, "sub": s}, device_id_type=MESH
            )

    own_rows = pl.ds(pl.multiple_of(ch * channels, channels), channels)
    own_half = archive_hbm.at[:, pl.ds(pl.multiple_of(ch * half, half), half)]
    own_list = lists_ref.at[me]
    loads = [
        pltpu.make_async_copy(source, target, load_sems.at[at])
        for at, (source, target) in enumerate(
            (
                (precision_hbm, precision_ref),
                (tail_hbm, tail_ref),
                (own_half, raw_ref.at[own_rows, :]),
                (tiles_hbm.at[0, 0], own_list),
            )
        )
    ]
    for load in loads:
        load.start()
    each_owner(announce)
    pl.semaphore_wait(barrier, (tm + 1) * (sub + 1))

    swap = send(
        archive_hbm.at[:, pl.ds(pl.multiple_of(other * half, half), half)],
        raw_ref.at[own_rows, :],
        raw_sems.at[0],
        raw_sems.at[1],
        {"ch": other},
    )
    swap.start()

    def direct(rank, t, s):
        return send(
            tiles_hbm.at[0, 0],
            own_list,
            list_send.at[rank],
            list_recv.at[me],
            {"tm": t, "sub": s},
        )

    def answer(rank, t, s):
        @pl.when(below(rank, t, s))
        def _():
            pl.semaphore_signal(
                here_sems.at[me], inc=1, device_id={"tm": t, "sub": s}, device_id_type=MESH
            )
            direct(rank, t, s).start()

    each_owner(answer)
    for load in loads[:2]:
        load.wait()
    factor = precision_ref[...]
    series_ref[last] = jnp.zeros((2 * channels, LANES), jnp.bfloat16)
    series_ref[last, :, : M - 1] = whiten(factor, tail_ref[...])
    for load in loads[2:]:
        load.wait()
    swap.wait_recv()

    def chunk(owner, part):
        return series_ref.at[pl.ds((owner * 2 + part) * tiles, tiles)]

    mine = chunk(tm, ch)
    whitened = whiten(factor, raw_ref[...])
    for k in range(tiles):
        series_ref[(tm * 2 + ch) * tiles + k] = whitened[:, k * LANES : (k + 1) * LANES]

    def along_time(t):
        return send(mine, mine, time_send.at[t], time_recv.at[tm], {"tm": t})

    to_pair = []

    def forward(held):
        step = len(to_pair)
        copy = send(held, held, pair_send.at[step], pair_recv.at[step], {"ch": other})
        to_pair.append(copy)
        copy.start()

    for t in range(n_tm):
        pl.when(t < tm)(along_time(t).start)
    forward(mine)
    for t in range(1, n_tm):

        @pl.when(t > tm)
        def _():
            pl.semaphore_wait(here_sems.at[t * n_sub + sub], 1)
            along_time(t).start()
            for s in range(n_sub):
                pl.when(s <= sub)(direct(t * n_sub + s, t, s).start)

    def list_up(rank, t, s):
        @pl.when(above(rank, t, s) & (s != sub))
        def _():
            pl.semaphore_wait(here_sems.at[rank], 1)
            direct(rank, t, s).start()
            for back in range(n_tm):
                pl.when((t == tm) & (back < tm))(direct(back * n_sub + s, back, s).start)

    each_owner(list_up)

    def landed(rank):
        held = lists_ref.at[rank]
        return send(held, held, list_send.at[0], list_recv.at[rank], {"ch": other})

    own_tile = me * (span // n_sub // LANES)
    early = (sub != n_sub - 1) | (tm == 0) | (tm == n_tm - 1)

    def prepare():
        own_columns(series_ref, own_tile, mine_ref, norms_ref)

    for step in range(1, n_tm):
        source = step + ((tm + n_tm - step) // n_tm) * (tm - 2 * step)
        held = chunk(source, ch)
        send(held, held, time_send.at[0], time_recv.at[source], {"ch": other}).wait_recv()
        forward(held)
        if step == 1:
            for copy in to_pair:
                copy.wait_recv()
            pl.when(early)(prepare)
    each_owner(lambda rank, t, s: pl.when(rank != me)(landed(rank).wait_recv))
    keep = pltpu.make_async_copy(lists_ref, lists_smem, load_sems.at[0])
    keep.start()
    swap.wait_send()
    for t in range(n_tm):
        pl.when(t != tm)(along_time(t).wait_send)
    each_owner(lambda rank, t, s: pl.when(rank != me)(direct(rank, t, s).wait_send))
    for copy in to_pair:
        copy.wait_send()
    for copy in to_pair[2:]:
        copy.wait_recv()
    pl.when(jnp.logical_not(early))(prepare)
    keep.wait()


def match_kernel(
    n_sub,
    series_ref,
    lists_smem,
    mine_ref,
    norms_ref,
    out_ref,
    work_smem,
    lagged_ref,
    wide_ref,
    products_ref,
    best_ref,
):
    units, unit_cols, _ = mine_ref.shape
    n_tiles = unit_cols // LANES
    unit = unit_cols - M
    per_block = TS // LANES
    rows = TS + M
    tm, ch = lax.axis_index("tm"), lax.axis_index("ch")
    me = tm * n_sub + lax.axis_index("sub")
    share = jnp.where(tm == 0, 1 - ch, ch)
    own_tile = me * (units * unit // LANES)
    for u in range(units):
        for s in range(PAIRED):
            best_ref[s, u] = jnp.full((8, unit_cols), jnp.inf, jnp.float32)
    lane = lax.broadcasted_iota(jnp.int32, (8, LANES), 1)
    own_at = [((lane // STEP) * n_tiles + t) * STEP + lane % STEP for t in range(n_tiles)]
    sublane = lax.broadcasted_iota(jnp.int32, (8, LANES), 0)

    owners = lists_smem.shape[0]

    def scan(owner, found):
        for slot in range(SLOTS):
            row_block, col_block = lists_smem[owner, slot, 0], lists_smem[owner, slot, 1]
            for u in range(units):
                block = (own_tile * LANES + u * unit) // TS
                work_smem[found] = (row_block + col_block - block) * units + u
                hit = (row_block == block) | (col_block == block)
                found = found + hit.astype(jnp.int32)
        return found

    if owners <= 16:
        found = jnp.int32(0)
        for owner in range(owners):
            found = scan(owner, found)
    else:
        found = lax.fori_loop(0, owners, scan, jnp.int32(0))

    def ahead(tiles, at):
        turn = at // n_tiles
        tile = tiles[at % n_tiles]
        return tile if turn == 0 else pltpu.roll(tile, LANES - turn * STEP, axis=1)

    def keep_apart(s, offset):
        for g in range(lines // STEP):
            if g % (M // STEP) < JOIN:
                for at in range(g * STEP, (g + 1) * STEP, 8):
                    for t in range(n_tiles):
                        here = (s, pl.ds(at, 8), pl.ds(t * LANES, LANES))
                        apart = (sublane + (at + offset)) - own_at[t]
                        products_ref[here] = jnp.where(
                            jnp.abs(apart) < EXCL, jnp.inf, products_ref[here]
                        )

    def reduce(s, u):
        low = [best_ref[s, u, :, t * LANES : (t + 1) * LANES] for t in range(n_tiles)]
        for part in range(0, STEP, 8):
            sums = {}
            for g in range(lines // STEP):
                at = g * STEP + part
                sums[JOIN, g] = [
                    products_ref[s, at : at + 8, t * LANES : (t + 1) * LANES] for t in range(n_tiles)
                ]
                first, size = g, JOIN
                while size < M // STEP and first >= size:
                    first -= size
                    early, late = sums[size, first], sums[size, first + size]
                    sums[2 * size, first] = [
                        early[t] + ahead(late, t + size) for t in range(n_tiles)
                    ]
                    size *= 2
                if size == M // STEP:
                    at = first * STEP + part
                    wide = wide_ref[s, at : at + 8, :]
                    for t in range(n_tiles):
                        low[t] = jnp.minimum(low[t], sums[size, first][t] + wide)
        for t in range(n_tiles):
            best_ref[s, u, :, t * LANES : (t + 1) * LANES] = low[t]

    lines = products_ref.shape[1]

    def shift(s, entry):
        lagged, norms = lag(series_ref, (entry // units) * per_block, rows // LANES, -2.0)
        place = 0
        for piece in lagged:
            lagged_ref[s, place : place + piece.shape[0], :] = piece
            place += piece.shape[0]
        for k in range(per_block):
            one = jnp.broadcast_to(norms[:1, k * LANES : (k + 1) * LANES], (LANES, LANES))
            wide_ref[s, k * LANES : (k + 1) * LANES, :] = jnp.transpose(one)

    def multiply(s, entry):
        longer = [lagged_ref[s, v * STEP : v * STEP + lines, :] for v in range(JOIN)]
        products_ref[s] = lax.dot_general(
            jnp.concatenate(longer, axis=1) if JOIN > 1 else longer[0],
            mine_ref[entry % units],
            (((1,), (1,)), ((), ())),
            preferred_element_type=jnp.float32,
        )

    def lower(s, entry):
        u = entry % units
        keep_apart(s, (entry // units) * TS - (own_tile * LANES + u * unit))
        reduce(s, u)

    share_count = (found + 1 - share) // 2

    def couple(at, _):
        entries = [
            work_smem[2 * (at * PAIRED + s) + share] for s in range(PAIRED)
        ]
        shift(0, entries[0])
        multiply(0, entries[0])
        shift(1, entries[1])
        multiply(1, entries[1])
        lower(0, entries[0])
        lower(1, entries[1])
        return 0

    lax.fori_loop(0, share_count // PAIRED, couple, 0)

    @pl.when(share_count % PAIRED == 1)
    def _():
        entry = work_smem[2 * (share_count - 1) + share]
        shift(0, entry)
        multiply(0, entry)
        lower(0, entry)

    group = lane // STEP
    for u in range(units):
        low = jnp.min(jnp.min(best_ref[:, u], axis=0), axis=0, keepdims=True)
        tiles = [
            jnp.broadcast_to(low[:, t * LANES : (t + 1) * LANES], (8, LANES)) for t in range(n_tiles)
        ]
        for k in range(unit // LANES):
            natural = None
            for g in range(LANES // STEP):
                q = k * (LANES // STEP) + g
                turn = (g - q // n_tiles) % (LANES // STEP)
                tile = tiles[q % n_tiles]
                tile = tile if turn == 0 else pltpu.roll(tile, turn * STEP, axis=1)
                natural = tile if natural is None else jnp.where(group == g, tile, natural)
            at = u * (unit // LANES) + k
            done = (natural[:1] + norms_ref[:1, at * LANES : (at + 1) * LANES]) * (1.0 / DEPTH)
            out_ref[at : at + 1, :] = done


def swap_kernel(mine_ref, theirs_ref, sems):
    other = {"ch": 1 - lax.axis_index("ch")}
    barrier = pltpu.get_barrier_semaphore()
    pl.semaphore_signal(barrier, inc=1, device_id=other, device_id_type=MESH)
    pl.semaphore_wait(barrier, 1)
    copy = pltpu.make_async_remote_copy(
        src_ref=mine_ref,
        dst_ref=theirs_ref,
        send_sem=sems.at[0],
        recv_sem=sems.at[1],
        device_id=other,
        device_id_type=MESH,
    )
    copy.start()
    copy.wait()


def lower_kernel(mine_ref, theirs_ref, out_ref):
    out_ref[...] = jnp.minimum(mine_ref[...], theirs_ref[...])


def body(archive, tail, precision, tile_list):
    n_tm, n_sub = lax.axis_size("tm"), lax.axis_size("sub")
    owners = n_tm * n_sub
    channels, span = archive.shape
    piece = span // n_sub
    unit = min(piece, TS)
    units = piece // unit
    every = 2 * channels
    depth = STEP * every
    anywhere = pl.BlockSpec(memory_space=pltpu.HBM)
    inside = pl.BlockSpec(memory_space=pltpu.VMEM)
    scalars = pl.BlockSpec(memory_space=pltpu.SMEM)
    series, lists, own, norms = pl.pallas_call(
        functools.partial(gather_kernel, n_tm, n_sub),
        out_shape=[
            pltpu.VMEM((n_tm * span // LANES + 1, every, LANES), jnp.bfloat16),
            pltpu.SMEM((owners,) + tile_list.shape[2:], jnp.int32),
            pltpu.VMEM((units, unit + M, JOIN * depth), jnp.bfloat16),
            pltpu.VMEM((8, piece + M), jnp.float32),
        ],
        in_specs=[anywhere] * 4,
        out_specs=[inside, scalars, inside, inside],
        scratch_shapes=[
            pltpu.VMEM((owners,) + tile_list.shape[2:], jnp.int32),
            pltpu.VMEM(tail.shape, jnp.float32),
            pltpu.VMEM(precision.shape, jnp.float32),
            pltpu.VMEM((every, span // 2), jnp.float32),
            pltpu.SemaphoreType.DMA((4,)),
            pltpu.SemaphoreType.DMA((2,)),
            pltpu.SemaphoreType.DMA((n_tm,)),
            pltpu.SemaphoreType.DMA((n_tm,)),
            pltpu.SemaphoreType.DMA((n_tm,)),
            pltpu.SemaphoreType.DMA((n_tm,)),
            pltpu.SemaphoreType.DMA((owners,)),
            pltpu.SemaphoreType.DMA((owners,)),
            pltpu.SemaphoreType.REGULAR((owners,)),
        ],
        compiler_params=pltpu.CompilerParams(
            collective_id=0, has_side_effects=True, vmem_limit_bytes=62 * 2**20
        ),
    )(tile_list, archive, tail, precision)
    series, own, norms = [
        pltpu.with_memory_space_constraint(array, pltpu.VMEM) for array in (series, own, norms)
    ]
    lists = pltpu.with_memory_space_constraint(lists, pltpu.SMEM)
    shape = (piece // LANES, LANES)
    mine = pl.pallas_call(
        functools.partial(match_kernel, n_sub),
        out_shape=pltpu.VMEM(shape, jnp.float32),
        in_specs=[inside, scalars, inside, inside],
        out_specs=inside,
        scratch_shapes=[
            pltpu.SMEM((owners * SLOTS * units + 1,), jnp.int32),
            pltpu.VMEM((PAIRED, TS + M, depth), jnp.bfloat16),
            pltpu.VMEM((PAIRED, TS, LANES), jnp.float32),
            pltpu.VMEM((PAIRED, TS + M - JOIN * STEP, unit + M), jnp.float32),
            pltpu.VMEM((PAIRED, units, 8, unit + M), jnp.float32),
        ],
        compiler_params=pltpu.CompilerParams(vmem_limit_bytes=32 * 2**20),
    )(series, lists, own, norms)
    mine = pltpu.with_memory_space_constraint(mine, pltpu.VMEM)
    theirs = pl.pallas_call(
        swap_kernel,
        out_shape=pltpu.VMEM(shape, jnp.float32),
        in_specs=[inside],
        out_specs=inside,
        scratch_shapes=[pltpu.SemaphoreType.DMA((2,))],
        compiler_params=pltpu.CompilerParams(
            collective_id=1, has_side_effects=True, vmem_limit_bytes=16 * 2**20
        ),
    )(mine)
    theirs = pltpu.with_memory_space_constraint(theirs, pltpu.VMEM)
    out = pl.pallas_call(
        lower_kernel,
        out_shape=jax.ShapeDtypeStruct(shape, jnp.float32),
        in_specs=[inside] * 2,
        out_specs=inside,
        compiler_params=pltpu.CompilerParams(vmem_limit_bytes=16 * 2**20),
    )(mine, theirs)
    return out.reshape(-1)


def solution(mesh):
    placed = (P("ch", ("grp", "tm")), P(None, "grp"), P(), P(("grp", "tm"), "sub", None, None))
    return jax.shard_map(
        body, mesh=mesh, in_specs=placed, out_specs=P(("grp", "tm", "sub")), check_vma=False
    )
```

```python
import functools

import jax
import jax.numpy as jnp
from jax import lax
from jax.experimental import pallas as pl
from jax.experimental.pallas import tpu as pltpu
from jax.sharding import PartitionSpec as P

M = 128
TS = 512
SLOTS = 2
DEPTH = 2048
EXCL = 32
LANES = 128
STEP = 16
JOIN = 2
PAIRED = 3
MESH = pl.DeviceIdType.MESH


def whiten(factor, samples):
    return jnp.dot(
        factor, samples, precision=lax.Precision.HIGHEST, preferred_element_type=jnp.float32
    ).astype(jnp.bfloat16)


def lag(series_ref, first_tile, count, scale):
    channels = series_ref.shape[1]
    pieces = [series_ref[first_tile + k].astype(jnp.float32) for k in range(count)]
    segment = jnp.concatenate(pieces, axis=1)
    width = count * LANES
    column = lax.broadcasted_iota(jnp.int32, (channels, LANES), 1)
    turned = {}

    def turn(k, l):
        k = min(k, count - 1)
        if (k, l) not in turned:
            turned[k, l] = pieces[k] if l == 0 else pltpu.roll(pieces[k], LANES - l, axis=1)
        return turned[k, l]

    def moved(k, l):
        here = turn(k, l)
        here = here if l == 0 else jnp.where(column < LANES - l, here, turn(k + 1, l))
        return here.astype(jnp.bfloat16)

    near = []
    for at in range(0, count, 2):
        tiles = range(at, min(at + 2, count))
        hankel = jnp.concatenate(
            [jnp.concatenate([moved(k, l) for k in tiles], axis=1) for l in range(8)], axis=0
        )
        size = len(tiles) * LANES
        unit_matrix = jnp.where(
            lax.broadcasted_iota(jnp.int32, (size, size), 0)
            == lax.broadcasted_iota(jnp.int32, (size, size), 1),
            scale,
            0.0,
        ).astype(jnp.bfloat16)
        near.append(
            lax.dot_general(
                unit_matrix, hankel, (((1,), (1,)), ((), ())), preferred_element_type=jnp.float32
            )
        )
    lagged = []
    for at, piece in enumerate(near):
        after = near[min(at + 1, len(near) - 1)]
        late = jnp.concatenate([piece[8:], after[:8]], axis=0)
        lagged.append(
            jnp.concatenate([piece.astype(jnp.bfloat16), late.astype(jnp.bfloat16)], axis=1)
        )
    norms = jnp.broadcast_to(jnp.sum(segment * segment, axis=0, keepdims=True), (8, width))
    shift = 1
    while shift < M:
        norms = norms + pltpu.roll(norms, width - shift, axis=1)
        shift *= 2
    return lagged, norms


def own_columns(series_ref, own_tile, mine_ref, norms_ref):
    units, unit_cols, joined = mine_ref.shape
    depth = joined // JOIN
    n_tiles = unit_cols // LANES
    unit = unit_cols - M
    lagged, norms_ref[...] = lag(series_ref, own_tile, units * unit // LANES + 1, 1.0)
    groups = [piece[at : at + STEP] for piece in lagged for at in range(0, piece.shape[0], STEP)]
    for u in range(units):
        for q in range(unit_cols // STEP):
            place = ((q % n_tiles) * 8 + q // n_tiles) * STEP
            for v in range(JOIN):
                at = min(u * unit // STEP + q + v, len(groups) - 1)
                mine_ref[u, place : place + STEP, v * depth : (v + 1) * depth] = groups[at]


def gather_kernel(
    n_tm,
    n_sub,
    tiles_hbm,
    archive_hbm,
    tail_hbm,
    precision_hbm,
    series_ref,
    lists_smem,
    mine_ref,
    norms_ref,
    lists_ref,
    tail_ref,
    precision_ref,
    raw_ref,
    load_sems,
    raw_sems,
    time_send,
    time_recv,
    pair_send,
    pair_recv,
    list_send,
    list_recv,
    here_sems,
):
    tm, sub, ch = lax.axis_index("tm"), lax.axis_index("sub"), lax.axis_index("ch")
    other = 1 - ch
    owners = n_tm * n_sub
    me = tm * n_sub + sub
    channels, span = archive_hbm.shape
    half = span // 2
    tiles = half // LANES
    last = n_tm * span // LANES

    def send(source, target, sem, landed, device):
        return pltpu.make_async_remote_copy(
            src_ref=source,
            dst_ref=target,
            send_sem=sem,
            recv_sem=landed,
            device_id=device,
            device_id_type=MESH,
        )

    def each_owner(action):
        if owners <= 16:
            for rank in range(owners):
                action(rank, rank // n_sub, rank % n_sub)
        else:
            lax.fori_loop(
                0, owners, lambda rank, _: (action(rank, rank // n_sub, rank % n_sub), 0)[1], 0
            )

    def above(rank, t, s):
        return (t >= tm) & (s >= sub) & (rank != me)

    def below(rank, t, s):
        return (t <= tm) & (s <= sub) & (rank != me)

    barrier = pltpu.get_barrier_semaphore()
    pl.semaphore_signal(barrier, inc=1, device_id={"ch": other}, device_id_type=MESH)

    def announce(rank, t, s):
        @pl.when(above(rank, t, s))
        def _():
            pl.semaphore_signal(
                barrier, inc=1, device_id={"tm": t, "sub": s}, device_id_type=MESH
            )

    own_rows = pl.ds(pl.multiple_of(ch * channels, channels), channels)
    own_half = archive_hbm.at[:, pl.ds(pl.multiple_of(ch * half, half), half)]
    own_list = lists_ref.at[me]
    loads = [
        pltpu.make_async_copy(source, target, load_sems.at[at])
        for at, (source, target) in enumerate(
            (
                (precision_hbm, precision_ref),
                (tail_hbm, tail_ref),
                (own_half, raw_ref.at[own_rows, :]),
                (tiles_hbm.at[0, 0], own_list),
            )
        )
    ]
    for load in loads:
        load.start()
    each_owner(announce)
    pl.semaphore_wait(barrier, (tm + 1) * (sub + 1))

    swap = send(
        archive_hbm.at[:, pl.ds(pl.multiple_of(other * half, half), half)],
        raw_ref.at[own_rows, :],
        raw_sems.at[0],
        raw_sems.at[1],
        {"ch": other},
    )
    swap.start()

    def direct(rank, t, s):
        return send(
            tiles_hbm.at[0, 0],
            own_list,
            list_send.at[rank],
            list_recv.at[me],
            {"tm": t, "sub": s},
        )

    def answer(rank, t, s):
        @pl.when(below(rank, t, s))
        def _():
            pl.semaphore_signal(
                here_sems.at[me], inc=1, device_id={"tm": t, "sub": s}, device_id_type=MESH
            )
            direct(rank, t, s).start()

    each_owner(answer)
    for load in loads[:2]:
        load.wait()
    factor = precision_ref[...]
    series_ref[last] = jnp.zeros((2 * channels, LANES), jnp.bfloat16)
    series_ref[last, :, : M - 1] = whiten(factor, tail_ref[...])
    for load in loads[2:]:
        load.wait()
    swap.wait_recv()

    def chunk(owner, part):
        return series_ref.at[pl.ds((owner * 2 + part) * tiles, tiles)]

    mine = chunk(tm, ch)
    whitened = whiten(factor, raw_ref[...])
    for k in range(tiles):
        series_ref[(tm * 2 + ch) * tiles + k] = whitened[:, k * LANES : (k + 1) * LANES]

    def along_time(t):
        return send(mine, mine, time_send.at[t], time_recv.at[tm], {"tm": t})

    to_pair = []

    def forward(held):
        step = len(to_pair)
        copy = send(held, held, pair_send.at[step], pair_recv.at[step], {"ch": other})
        to_pair.append(copy)
        copy.start()

    for t in range(n_tm):
        pl.when(t < tm)(along_time(t).start)
    forward(mine)
    for t in range(1, n_tm):

        @pl.when(t > tm)
        def _():
            pl.semaphore_wait(here_sems.at[t * n_sub + sub], 1)
            along_time(t).start()
            for s in range(n_sub):
                pl.when(s <= sub)(direct(t * n_sub + s, t, s).start)

    def list_up(rank, t, s):
        @pl.when(above(rank, t, s) & (s != sub))
        def _():
            pl.semaphore_wait(here_sems.at[rank], 1)
            direct(rank, t, s).start()
            for back in range(n_tm):
                pl.when((t == tm) & (back < tm))(direct(back * n_sub + s, back, s).start)

    each_owner(list_up)

    def landed(rank):
        held = lists_ref.at[rank]
        return send(held, held, list_send.at[0], list_recv.at[rank], {"ch": other})

    own_tile = me * (span // n_sub // LANES)
    early = (sub != n_sub - 1) | (tm == 0) | (tm == n_tm - 1)

    def prepare():
        own_columns(series_ref, own_tile, mine_ref, norms_ref)

    for step in range(1, n_tm):
        source = step + ((tm + n_tm - step) // n_tm) * (tm - 2 * step)
        held = chunk(source, ch)
        send(held, held, time_send.at[0], time_recv.at[source], {"ch": other}).wait_recv()
        forward(held)
        if step == 1:
            for copy in to_pair:
                copy.wait_recv()
            pl.when(early)(prepare)
    each_owner(lambda rank, t, s: pl.when(rank != me)(landed(rank).wait_recv))
    keep = pltpu.make_async_copy(lists_ref, lists_smem, load_sems.at[0])
    keep.start()
    swap.wait_send()
    for t in range(n_tm):
        pl.when(t != tm)(along_time(t).wait_send)
    each_owner(lambda rank, t, s: pl.when(rank != me)(direct(rank, t, s).wait_send))
    for copy in to_pair:
        copy.wait_send()
    for copy in to_pair[2:]:
        copy.wait_recv()
    pl.when(jnp.logical_not(early))(prepare)
    keep.wait()


def match_kernel(
    n_sub,
    series_ref,
    lists_smem,
    mine_ref,
    norms_ref,
    out_ref,
    work_smem,
    lagged_ref,
    wide_ref,
    products_ref,
    best_ref,
):
    units, unit_cols, _ = mine_ref.shape
    n_tiles = unit_cols // LANES
    unit = unit_cols - M
    per_block = TS // LANES
    rows = TS + M
    tm, ch = lax.axis_index("tm"), lax.axis_index("ch")
    me = tm * n_sub + lax.axis_index("sub")
    share = jnp.where(tm == 0, 1 - ch, ch)
    own_tile = me * (units * unit // LANES)
    for u in range(units):
        for s in range(PAIRED):
            best_ref[s, u] = jnp.full((8, unit_cols), jnp.inf, jnp.float32)
    lane = lax.broadcasted_iota(jnp.int32, (8, LANES), 1)
    own_at = [((lane // STEP) * n_tiles + t) * STEP + lane % STEP for t in range(n_tiles)]
    sublane = lax.broadcasted_iota(jnp.int32, (8, LANES), 0)

    owners = lists_smem.shape[0]

    def scan(owner, found):
        for slot in range(SLOTS):
            row_block, col_block = lists_smem[owner, slot, 0], lists_smem[owner, slot, 1]
            for u in range(units):
                block = (own_tile * LANES + u * unit) // TS
                work_smem[found] = (row_block + col_block - block) * units + u
                hit = (row_block == block) | (col_block == block)
                found = found + hit.astype(jnp.int32)
        return found

    if owners <= 16:
        found = jnp.int32(0)
        for owner in range(owners):
            found = scan(owner, found)
    else:
        found = lax.fori_loop(0, owners, scan, jnp.int32(0))

    def ahead(tiles, at):
        turn = at // n_tiles
        tile = tiles[at % n_tiles]
        return tile if turn == 0 else pltpu.roll(tile, LANES - turn * STEP, axis=1)

    def keep_apart(s, offset):
        for g in range(lines // STEP):
            if g % (M // STEP) < JOIN:
                for at in range(g * STEP, (g + 1) * STEP, 8):
                    for t in range(n_tiles):
                        here = (s, pl.ds(at, 8), pl.ds(t * LANES, LANES))
                        apart = (sublane + (at + offset)) - own_at[t]
                        products_ref[here] = jnp.where(
                            jnp.abs(apart) < EXCL, jnp.inf, products_ref[here]
                        )

    def reduce(s, u):
        low = [best_ref[s, u, :, t * LANES : (t + 1) * LANES] for t in range(n_tiles)]
        for part in range(0, STEP, 8):
            sums = {}
            for g in range(lines // STEP):
                at = g * STEP + part
                sums[JOIN, g] = [
                    products_ref[s, at : at + 8, t * LANES : (t + 1) * LANES] for t in range(n_tiles)
                ]
                first, size = g, JOIN
                while size < M // STEP and first >= size:
                    first -= size
                    early, late = sums[size, first], sums[size, first + size]
                    sums[2 * size, first] = [
                        early[t] + ahead(late, t + size) for t in range(n_tiles)
                    ]
                    size *= 2
                if size == M // STEP:
                    at = first * STEP + part
                    wide = wide_ref[s, at : at + 8, :]
                    for t in range(n_tiles):
                        low[t] = jnp.minimum(low[t], sums[size, first][t] + wide)
        for t in range(n_tiles):
            best_ref[s, u, :, t * LANES : (t + 1) * LANES] = low[t]

    lines = products_ref.shape[1]

    def shift(s, entry):
        lagged, norms = lag(series_ref, (entry // units) * per_block, rows // LANES, -2.0)
        place = 0
        for piece in lagged:
            lagged_ref[s, place : place + piece.shape[0], :] = piece
            place += piece.shape[0]
        for k in range(per_block):
            one = jnp.broadcast_to(norms[:1, k * LANES : (k + 1) * LANES], (LANES, LANES))
            wide_ref[s, k * LANES : (k + 1) * LANES, :] = jnp.transpose(one)

    def multiply(s, entry):
        longer = [lagged_ref[s, v * STEP : v * STEP + lines, :] for v in range(JOIN)]
        products_ref[s] = lax.dot_general(
            jnp.concatenate(longer, axis=1) if JOIN > 1 else longer[0],
            mine_ref[entry % units],
            (((1,), (1,)), ((), ())),
            preferred_element_type=jnp.float32,
        )

    def lower(s, entry):
        u = entry % units
        keep_apart(s, (entry // units) * TS - (own_tile * LANES + u * unit))
        reduce(s, u)

    share_count = (found + 1 - share) // 2

    def together(first, count):
        entries = [work_smem[2 * (first + s) + share] for s in range(count)]
        for s in range(count):
            shift(s, entries[s])
            multiply(s, entries[s])
        for s in range(count):
            lower(s, entries[s])

    triples = jnp.where(
        share_count % 3 == 1, jnp.maximum(share_count // 3 - 1, 0), share_count // 3
    )
    rest = share_count - 3 * triples

    def triple(at, _):
        together(3 * at, 3)
        return 0

    def couple(at, _):
        together(3 * triples + 2 * at, 2)
        return 0

    lax.fori_loop(0, triples, triple, 0)
    lax.fori_loop(0, rest // 2, couple, 0)

    @pl.when(rest % 2 == 1)
    def _():
        together(share_count - 1, 1)

    group = lane // STEP
    for u in range(units):
        low = jnp.min(jnp.min(best_ref[:, u], axis=0), axis=0, keepdims=True)
        tiles = [
            jnp.broadcast_to(low[:, t * LANES : (t + 1) * LANES], (8, LANES)) for t in range(n_tiles)
        ]
        for k in range(unit // LANES):
            natural = None
            for g in range(LANES // STEP):
                q = k * (LANES // STEP) + g
                turn = (g - q // n_tiles) % (LANES // STEP)
                tile = tiles[q % n_tiles]
                tile = tile if turn == 0 else pltpu.roll(tile, turn * STEP, axis=1)
                natural = tile if natural is None else jnp.where(group == g, tile, natural)
            at = u * (unit // LANES) + k
            done = (natural[:1] + norms_ref[:1, at * LANES : (at + 1) * LANES]) * (1.0 / DEPTH)
            out_ref[at : at + 1, :] = done


def swap_kernel(mine_ref, theirs_ref, sems):
    other = {"ch": 1 - lax.axis_index("ch")}
    barrier = pltpu.get_barrier_semaphore()
    pl.semaphore_signal(barrier, inc=1, device_id=other, device_id_type=MESH)
    pl.semaphore_wait(barrier, 1)
    copy = pltpu.make_async_remote_copy(
        src_ref=mine_ref,
        dst_ref=theirs_ref,
        send_sem=sems.at[0],
        recv_sem=sems.at[1],
        device_id=other,
        device_id_type=MESH,
    )
    copy.start()
    copy.wait()


def lower_kernel(mine_ref, theirs_ref, out_ref):
    out_ref[...] = jnp.minimum(mine_ref[...], theirs_ref[...])


def body(archive, tail, precision, tile_list):
    n_tm, n_sub = lax.axis_size("tm"), lax.axis_size("sub")
    owners = n_tm * n_sub
    channels, span = archive.shape
    piece = span // n_sub
    unit = min(piece, TS)
    units = piece // unit
    every = 2 * channels
    depth = STEP * every
    anywhere = pl.BlockSpec(memory_space=pltpu.HBM)
    inside = pl.BlockSpec(memory_space=pltpu.VMEM)
    scalars = pl.BlockSpec(memory_space=pltpu.SMEM)
    series, lists, own, norms = pl.pallas_call(
        functools.partial(gather_kernel, n_tm, n_sub),
        out_shape=[
            pltpu.VMEM((n_tm * span // LANES + 1, every, LANES), jnp.bfloat16),
            pltpu.SMEM((owners,) + tile_list.shape[2:], jnp.int32),
            pltpu.VMEM((units, unit + M, JOIN * depth), jnp.bfloat16),
            pltpu.VMEM((8, piece + M), jnp.float32),
        ],
        in_specs=[anywhere] * 4,
        out_specs=[inside, scalars, inside, inside],
        scratch_shapes=[
            pltpu.VMEM((owners,) + tile_list.shape[2:], jnp.int32),
            pltpu.VMEM(tail.shape, jnp.float32),
            pltpu.VMEM(precision.shape, jnp.float32),
            pltpu.VMEM((every, span // 2), jnp.float32),
            pltpu.SemaphoreType.DMA((4,)),
            pltpu.SemaphoreType.DMA((2,)),
            pltpu.SemaphoreType.DMA((n_tm,)),
            pltpu.SemaphoreType.DMA((n_tm,)),
            pltpu.SemaphoreType.DMA((n_tm,)),
            pltpu.SemaphoreType.DMA((n_tm,)),
            pltpu.SemaphoreType.DMA((owners,)),
            pltpu.SemaphoreType.DMA((owners,)),
            pltpu.SemaphoreType.REGULAR((owners,)),
        ],
        compiler_params=pltpu.CompilerParams(
            collective_id=0, has_side_effects=True, vmem_limit_bytes=62 * 2**20
        ),
    )(tile_list, archive, tail, precision)
    series, own, norms = [
        pltpu.with_memory_space_constraint(array, pltpu.VMEM) for array in (series, own, norms)
    ]
    lists = pltpu.with_memory_space_constraint(lists, pltpu.SMEM)
    shape = (piece // LANES, LANES)
    mine = pl.pallas_call(
        functools.partial(match_kernel, n_sub),
        out_shape=pltpu.VMEM(shape, jnp.float32),
        in_specs=[inside, scalars, inside, inside],
        out_specs=inside,
        scratch_shapes=[
            pltpu.SMEM((owners * SLOTS * units + 1,), jnp.int32),
            pltpu.VMEM((PAIRED, TS + M, depth), jnp.bfloat16),
            pltpu.VMEM((PAIRED, TS, LANES), jnp.float32),
            pltpu.VMEM((PAIRED, TS + M - JOIN * STEP, unit + M), jnp.float32),
            pltpu.VMEM((PAIRED, units, 8, unit + M), jnp.float32),
        ],
        compiler_params=pltpu.CompilerParams(vmem_limit_bytes=32 * 2**20),
    )(series, lists, own, norms)
    mine = pltpu.with_memory_space_constraint(mine, pltpu.VMEM)
    theirs = pl.pallas_call(
        swap_kernel,
        out_shape=pltpu.VMEM(shape, jnp.float32),
        in_specs=[inside],
        out_specs=inside,
        scratch_shapes=[pltpu.SemaphoreType.DMA((2,))],
        compiler_params=pltpu.CompilerParams(
            collective_id=1, has_side_effects=True, vmem_limit_bytes=16 * 2**20
        ),
    )(mine)
    theirs = pltpu.with_memory_space_constraint(theirs, pltpu.VMEM)
    out = pl.pallas_call(
        lower_kernel,
        out_shape=jax.ShapeDtypeStruct(shape, jnp.float32),
        in_specs=[inside] * 2,
        out_specs=inside,
        compiler_params=pltpu.CompilerParams(vmem_limit_bytes=16 * 2**20),
    )(mine, theirs)
    return out.reshape(-1)


def solution(mesh):
    placed = (P("ch", ("grp", "tm")), P(None, "grp"), P(), P(("grp", "tm"), "sub", None, None))
    return jax.shard_map(
        body, mesh=mesh, in_specs=placed, out_specs=P(("grp", "tm", "sub")), check_vma=False
    )
```

```python
import functools

import jax
import jax.numpy as jnp
from jax import lax
from jax.experimental import pallas as pl
from jax.experimental.pallas import tpu as pltpu
from jax.sharding import PartitionSpec as P

M = 128
TS = 512
SLOTS = 2
DEPTH = 2048
EXCL = 32
LANES = 128
STEP = 16
JOIN = 2
PAIRED = 4
MESH = pl.DeviceIdType.MESH


def whiten(factor, samples):
    return jnp.dot(
        factor, samples, precision=lax.Precision.HIGHEST, preferred_element_type=jnp.float32
    ).astype(jnp.bfloat16)


def lag(series_ref, first_tile, count, scale):
    channels = series_ref.shape[1]
    pieces = [series_ref[first_tile + k].astype(jnp.float32) for k in range(count)]
    segment = jnp.concatenate(pieces, axis=1)
    width = count * LANES
    column = lax.broadcasted_iota(jnp.int32, (channels, LANES), 1)
    turned = {}

    def turn(k, l):
        k = min(k, count - 1)
        if (k, l) not in turned:
            turned[k, l] = pieces[k] if l == 0 else pltpu.roll(pieces[k], LANES - l, axis=1)
        return turned[k, l]

    def moved(k, l):
        here = turn(k, l)
        here = here if l == 0 else jnp.where(column < LANES - l, here, turn(k + 1, l))
        return here.astype(jnp.bfloat16)

    near = []
    for at in range(0, count, 2):
        tiles = range(at, min(at + 2, count))
        hankel = jnp.concatenate(
            [jnp.concatenate([moved(k, l) for k in tiles], axis=1) for l in range(8)], axis=0
        )
        size = len(tiles) * LANES
        unit_matrix = jnp.where(
            lax.broadcasted_iota(jnp.int32, (size, size), 0)
            == lax.broadcasted_iota(jnp.int32, (size, size), 1),
            scale,
            0.0,
        ).astype(jnp.bfloat16)
        near.append(
            lax.dot_general(
                unit_matrix, hankel, (((1,), (1,)), ((), ())), preferred_element_type=jnp.float32
            )
        )
    lagged = []
    for at, piece in enumerate(near):
        after = near[min(at + 1, len(near) - 1)]
        late = jnp.concatenate([piece[8:], after[:8]], axis=0)
        lagged.append(
            jnp.concatenate([piece.astype(jnp.bfloat16), late.astype(jnp.bfloat16)], axis=1)
        )
    norms = jnp.broadcast_to(jnp.sum(segment * segment, axis=0, keepdims=True), (8, width))
    shift = 1
    while shift < M:
        norms = norms + pltpu.roll(norms, width - shift, axis=1)
        shift *= 2
    return lagged, norms


def own_columns(series_ref, own_tile, mine_ref, norms_ref):
    units, unit_cols, joined = mine_ref.shape
    depth = joined // JOIN
    n_tiles = unit_cols // LANES
    unit = unit_cols - M
    lagged, norms_ref[...] = lag(series_ref, own_tile, units * unit // LANES + 1, 1.0)
    groups = [piece[at : at + STEP] for piece in lagged for at in range(0, piece.shape[0], STEP)]
    for u in range(units):
        for q in range(unit_cols // STEP):
            place = ((q % n_tiles) * 8 + q // n_tiles) * STEP
            for v in range(JOIN):
                at = min(u * unit // STEP + q + v, len(groups) - 1)
                mine_ref[u, place : place + STEP, v * depth : (v + 1) * depth] = groups[at]


def gather_kernel(
    n_tm,
    n_sub,
    tiles_hbm,
    archive_hbm,
    tail_hbm,
    precision_hbm,
    series_ref,
    lists_smem,
    mine_ref,
    norms_ref,
    lists_ref,
    tail_ref,
    precision_ref,
    raw_ref,
    load_sems,
    raw_sems,
    time_send,
    time_recv,
    pair_send,
    pair_recv,
    list_send,
    list_recv,
    here_sems,
):
    tm, sub, ch = lax.axis_index("tm"), lax.axis_index("sub"), lax.axis_index("ch")
    other = 1 - ch
    owners = n_tm * n_sub
    me = tm * n_sub + sub
    channels, span = archive_hbm.shape
    half = span // 2
    tiles = half // LANES
    last = n_tm * span // LANES

    def send(source, target, sem, landed, device):
        return pltpu.make_async_remote_copy(
            src_ref=source,
            dst_ref=target,
            send_sem=sem,
            recv_sem=landed,
            device_id=device,
            device_id_type=MESH,
        )

    def each_owner(action):
        if owners <= 16:
            for rank in range(owners):
                action(rank, rank // n_sub, rank % n_sub)
        else:
            lax.fori_loop(
                0, owners, lambda rank, _: (action(rank, rank // n_sub, rank % n_sub), 0)[1], 0
            )

    def above(rank, t, s):
        return (t >= tm) & (s >= sub) & (rank != me)

    def below(rank, t, s):
        return (t <= tm) & (s <= sub) & (rank != me)

    barrier = pltpu.get_barrier_semaphore()
    pl.semaphore_signal(barrier, inc=1, device_id={"ch": other}, device_id_type=MESH)

    def announce(rank, t, s):
        @pl.when(above(rank, t, s))
        def _():
            pl.semaphore_signal(
                barrier, inc=1, device_id={"tm": t, "sub": s}, device_id_type=MESH
            )

    own_rows = pl.ds(pl.multiple_of(ch * channels, channels), channels)
    own_half = archive_hbm.at[:, pl.ds(pl.multiple_of(ch * half, half), half)]
    own_list = lists_ref.at[me]
    loads = [
        pltpu.make_async_copy(source, target, load_sems.at[at])
        for at, (source, target) in enumerate(
            (
                (precision_hbm, precision_ref),
                (tail_hbm, tail_ref),
                (own_half, raw_ref.at[own_rows, :]),
                (tiles_hbm.at[0, 0], own_list),
            )
        )
    ]
    for load in loads:
        load.start()
    each_owner(announce)
    pl.semaphore_wait(barrier, (tm + 1) * (sub + 1))

    swap = send(
        archive_hbm.at[:, pl.ds(pl.multiple_of(other * half, half), half)],
        raw_ref.at[own_rows, :],
        raw_sems.at[0],
        raw_sems.at[1],
        {"ch": other},
    )
    swap.start()

    def direct(rank, t, s):
        return send(
            tiles_hbm.at[0, 0],
            own_list,
            list_send.at[rank],
            list_recv.at[me],
            {"tm": t, "sub": s},
        )

    def answer(rank, t, s):
        @pl.when(below(rank, t, s))
        def _():
            pl.semaphore_signal(
                here_sems.at[me], inc=1, device_id={"tm": t, "sub": s}, device_id_type=MESH
            )
            direct(rank, t, s).start()

    each_owner(answer)
    for load in loads[:2]:
        load.wait()
    factor = precision_ref[...]
    series_ref[last] = jnp.zeros((2 * channels, LANES), jnp.bfloat16)
    series_ref[last, :, : M - 1] = whiten(factor, tail_ref[...])
    for load in loads[2:]:
        load.wait()
    swap.wait_recv()

    def chunk(owner, part):
        return series_ref.at[pl.ds((owner * 2 + part) * tiles, tiles)]

    mine = chunk(tm, ch)
    whitened = whiten(factor, raw_ref[...])
    for k in range(tiles):
        series_ref[(tm * 2 + ch) * tiles + k] = whitened[:, k * LANES : (k + 1) * LANES]

    def along_time(t):
        return send(mine, mine, time_send.at[t], time_recv.at[tm], {"tm": t})

    to_pair = []

    def forward(held):
        step = len(to_pair)
        copy = send(held, held, pair_send.at[step], pair_recv.at[step], {"ch": other})
        to_pair.append(copy)
        copy.start()

    for t in range(n_tm):
        pl.when(t < tm)(along_time(t).start)
    forward(mine)
    for t in range(1, n_tm):

        @pl.when(t > tm)
        def _():
            pl.semaphore_wait(here_sems.at[t * n_sub + sub], 1)
            along_time(t).start()
            for s in range(n_sub):
                pl.when(s <= sub)(direct(t * n_sub + s, t, s).start)

    def list_up(rank, t, s):
        @pl.when(above(rank, t, s) & (s != sub))
        def _():
            pl.semaphore_wait(here_sems.at[rank], 1)
            direct(rank, t, s).start()
            for back in range(n_tm):
                pl.when((t == tm) & (back < tm))(direct(back * n_sub + s, back, s).start)

    each_owner(list_up)

    def landed(rank):
        held = lists_ref.at[rank]
        return send(held, held, list_send.at[0], list_recv.at[rank], {"ch": other})

    own_tile = me * (span // n_sub // LANES)
    early = (sub != n_sub - 1) | (tm == 0) | (tm == n_tm - 1)

    def prepare():
        own_columns(series_ref, own_tile, mine_ref, norms_ref)

    for step in range(1, n_tm):
        source = step + ((tm + n_tm - step) // n_tm) * (tm - 2 * step)
        held = chunk(source, ch)
        send(held, held, time_send.at[0], time_recv.at[source], {"ch": other}).wait_recv()
        forward(held)
        if step == 1:
            for copy in to_pair:
                copy.wait_recv()
            pl.when(early)(prepare)
    each_owner(lambda rank, t, s: pl.when(rank != me)(landed(rank).wait_recv))
    keep = pltpu.make_async_copy(lists_ref, lists_smem, load_sems.at[0])
    keep.start()
    swap.wait_send()
    for t in range(n_tm):
        pl.when(t != tm)(along_time(t).wait_send)
    each_owner(lambda rank, t, s: pl.when(rank != me)(direct(rank, t, s).wait_send))
    for copy in to_pair:
        copy.wait_send()
    for copy in to_pair[2:]:
        copy.wait_recv()
    pl.when(jnp.logical_not(early))(prepare)
    keep.wait()


def match_kernel(
    n_sub,
    series_ref,
    lists_smem,
    mine_ref,
    norms_ref,
    out_ref,
    work_smem,
    lagged_ref,
    wide_ref,
    products_ref,
    best_ref,
):
    units, unit_cols, _ = mine_ref.shape
    n_tiles = unit_cols // LANES
    unit = unit_cols - M
    per_block = TS // LANES
    rows = TS + M
    tm, ch = lax.axis_index("tm"), lax.axis_index("ch")
    me = tm * n_sub + lax.axis_index("sub")
    share = jnp.where(tm == 0, 1 - ch, ch)
    own_tile = me * (units * unit // LANES)
    for u in range(units):
        for s in range(PAIRED):
            best_ref[s, u] = jnp.full((8, unit_cols), jnp.inf, jnp.float32)
    lane = lax.broadcasted_iota(jnp.int32, (8, LANES), 1)
    own_at = [((lane // STEP) * n_tiles + t) * STEP + lane % STEP for t in range(n_tiles)]
    sublane = lax.broadcasted_iota(jnp.int32, (8, LANES), 0)

    owners = lists_smem.shape[0]

    def scan(owner, found):
        for slot in range(SLOTS):
            row_block, col_block = lists_smem[owner, slot, 0], lists_smem[owner, slot, 1]
            for u in range(units):
                block = (own_tile * LANES + u * unit) // TS
                work_smem[found] = (row_block + col_block - block) * units + u
                hit = (row_block == block) | (col_block == block)
                found = found + hit.astype(jnp.int32)
        return found

    if owners <= 16:
        found = jnp.int32(0)
        for owner in range(owners):
            found = scan(owner, found)
    else:
        found = lax.fori_loop(0, owners, scan, jnp.int32(0))

    def ahead(tiles, at):
        turn = at // n_tiles
        tile = tiles[at % n_tiles]
        return tile if turn == 0 else pltpu.roll(tile, LANES - turn * STEP, axis=1)

    def keep_apart(s, offset):
        for g in range(lines // STEP):
            if g % (M // STEP) < JOIN:
                for at in range(g * STEP, (g + 1) * STEP, 8):
                    for t in range(n_tiles):
                        here = (s, pl.ds(at, 8), pl.ds(t * LANES, LANES))
                        apart = (sublane + (at + offset)) - own_at[t]
                        products_ref[here] = jnp.where(
                            jnp.abs(apart) < EXCL, jnp.inf, products_ref[here]
                        )

    def reduce(s, u):
        low = [best_ref[s, u, :, t * LANES : (t + 1) * LANES] for t in range(n_tiles)]
        for part in range(0, STEP, 8):
            sums = {}
            for g in range(lines // STEP):
                at = g * STEP + part
                sums[JOIN, g] = [
                    products_ref[s, at : at + 8, t * LANES : (t + 1) * LANES] for t in range(n_tiles)
                ]
                first, size = g, JOIN
                while size < M // STEP and first >= size:
                    first -= size
                    early, late = sums[size, first], sums[size, first + size]
                    sums[2 * size, first] = [
                        early[t] + ahead(late, t + size) for t in range(n_tiles)
                    ]
                    size *= 2
                if size == M // STEP:
                    at = first * STEP + part
                    wide = wide_ref[s, at : at + 8, :]
                    for t in range(n_tiles):
                        low[t] = jnp.minimum(low[t], sums[size, first][t] + wide)
        for t in range(n_tiles):
            best_ref[s, u, :, t * LANES : (t + 1) * LANES] = low[t]

    lines = products_ref.shape[1]

    def shift(s, entry):
        lagged, norms = lag(series_ref, (entry // units) * per_block, rows // LANES, -2.0)
        place = 0
        for piece in lagged:
            lagged_ref[s, place : place + piece.shape[0], :] = piece
            place += piece.shape[0]
        for k in range(per_block):
            one = jnp.broadcast_to(norms[:1, k * LANES : (k + 1) * LANES], (LANES, LANES))
            wide_ref[s, k * LANES : (k + 1) * LANES, :] = jnp.transpose(one)

    def multiply(s, entry):
        longer = [lagged_ref[s, v * STEP : v * STEP + lines, :] for v in range(JOIN)]
        products_ref[s] = lax.dot_general(
            jnp.concatenate(longer, axis=1) if JOIN > 1 else longer[0],
            mine_ref[entry % units],
            (((1,), (1,)), ((), ())),
            preferred_element_type=jnp.float32,
        )

    def lower(s, entry):
        u = entry % units
        keep_apart(s, (entry // units) * TS - (own_tile * LANES + u * unit))
        reduce(s, u)

    share_count = (found + 1 - share) // 2

    def together(first, count):
        entries = [work_smem[2 * (first + s) + share] for s in range(count)]
        for s in range(count):
            shift(s, entries[s])
            multiply(s, entries[s])
        for s in range(count):
            lower(s, entries[s])

    def four(at, _):
        together(4 * at, 4)
        return 0

    fours = share_count // 4
    lax.fori_loop(0, fours, four, 0)
    for count in (3, 2, 1):
        pl.when(share_count % 4 == count)(functools.partial(together, 4 * fours, count))

    group = lane // STEP
    for u in range(units):
        low = jnp.min(jnp.min(best_ref[:, u], axis=0), axis=0, keepdims=True)
        tiles = [
            jnp.broadcast_to(low[:, t * LANES : (t + 1) * LANES], (8, LANES)) for t in range(n_tiles)
        ]
        for k in range(unit // LANES):
            natural = None
            for g in range(LANES // STEP):
                q = k * (LANES // STEP) + g
                turn = (g - q // n_tiles) % (LANES // STEP)
                tile = tiles[q % n_tiles]
                tile = tile if turn == 0 else pltpu.roll(tile, turn * STEP, axis=1)
                natural = tile if natural is None else jnp.where(group == g, tile, natural)
            at = u * (unit // LANES) + k
            done = (natural[:1] + norms_ref[:1, at * LANES : (at + 1) * LANES]) * (1.0 / DEPTH)
            out_ref[at : at + 1, :] = done


def swap_kernel(mine_ref, theirs_ref, sems):
    other = {"ch": 1 - lax.axis_index("ch")}
    barrier = pltpu.get_barrier_semaphore()
    pl.semaphore_signal(barrier, inc=1, device_id=other, device_id_type=MESH)
    pl.semaphore_wait(barrier, 1)
    copy = pltpu.make_async_remote_copy(
        src_ref=mine_ref,
        dst_ref=theirs_ref,
        send_sem=sems.at[0],
        recv_sem=sems.at[1],
        device_id=other,
        device_id_type=MESH,
    )
    copy.start()
    copy.wait()


def lower_kernel(mine_ref, theirs_ref, out_ref):
    out_ref[...] = jnp.minimum(mine_ref[...], theirs_ref[...])


def body(archive, tail, precision, tile_list):
    n_tm, n_sub = lax.axis_size("tm"), lax.axis_size("sub")
    owners = n_tm * n_sub
    channels, span = archive.shape
    piece = span // n_sub
    unit = min(piece, TS)
    units = piece // unit
    every = 2 * channels
    depth = STEP * every
    anywhere = pl.BlockSpec(memory_space=pltpu.HBM)
    inside = pl.BlockSpec(memory_space=pltpu.VMEM)
    scalars = pl.BlockSpec(memory_space=pltpu.SMEM)
    series, lists, own, norms = pl.pallas_call(
        functools.partial(gather_kernel, n_tm, n_sub),
        out_shape=[
            pltpu.VMEM((n_tm * span // LANES + 1, every, LANES), jnp.bfloat16),
            pltpu.SMEM((owners,) + tile_list.shape[2:], jnp.int32),
            pltpu.VMEM((units, unit + M, JOIN * depth), jnp.bfloat16),
            pltpu.VMEM((8, piece + M), jnp.float32),
        ],
        in_specs=[anywhere] * 4,
        out_specs=[inside, scalars, inside, inside],
        scratch_shapes=[
            pltpu.VMEM((owners,) + tile_list.shape[2:], jnp.int32),
            pltpu.VMEM(tail.shape, jnp.float32),
            pltpu.VMEM(precision.shape, jnp.float32),
            pltpu.VMEM((every, span // 2), jnp.float32),
            pltpu.SemaphoreType.DMA((4,)),
            pltpu.SemaphoreType.DMA((2,)),
            pltpu.SemaphoreType.DMA((n_tm,)),
            pltpu.SemaphoreType.DMA((n_tm,)),
            pltpu.SemaphoreType.DMA((n_tm,)),
            pltpu.SemaphoreType.DMA((n_tm,)),
            pltpu.SemaphoreType.DMA((owners,)),
            pltpu.SemaphoreType.DMA((owners,)),
            pltpu.SemaphoreType.REGULAR((owners,)),
        ],
        compiler_params=pltpu.CompilerParams(
            collective_id=0, has_side_effects=True, vmem_limit_bytes=62 * 2**20
        ),
    )(tile_list, archive, tail, precision)
    series, own, norms = [
        pltpu.with_memory_space_constraint(array, pltpu.VMEM) for array in (series, own, norms)
    ]
    lists = pltpu.with_memory_space_constraint(lists, pltpu.SMEM)
    shape = (piece // LANES, LANES)
    mine = pl.pallas_call(
        functools.partial(match_kernel, n_sub),
        out_shape=pltpu.VMEM(shape, jnp.float32),
        in_specs=[inside, scalars, inside, inside],
        out_specs=inside,
        scratch_shapes=[
            pltpu.SMEM((owners * SLOTS * units + 1,), jnp.int32),
            pltpu.VMEM((PAIRED, TS + M, depth), jnp.bfloat16),
            pltpu.VMEM((PAIRED, TS, LANES), jnp.float32),
            pltpu.VMEM((PAIRED, TS + M - JOIN * STEP, unit + M), jnp.float32),
            pltpu.VMEM((PAIRED, units, 8, unit + M), jnp.float32),
        ],
        compiler_params=pltpu.CompilerParams(vmem_limit_bytes=32 * 2**20),
    )(series, lists, own, norms)
    mine = pltpu.with_memory_space_constraint(mine, pltpu.VMEM)
    theirs = pl.pallas_call(
        swap_kernel,
        out_shape=pltpu.VMEM(shape, jnp.float32),
        in_specs=[inside],
        out_specs=inside,
        scratch_shapes=[pltpu.SemaphoreType.DMA((2,))],
        compiler_params=pltpu.CompilerParams(
            collective_id=1, has_side_effects=True, vmem_limit_bytes=16 * 2**20
        ),
    )(mine)
    theirs = pltpu.with_memory_space_constraint(theirs, pltpu.VMEM)
    out = pl.pallas_call(
        lower_kernel,
        out_shape=jax.ShapeDtypeStruct(shape, jnp.float32),
        in_specs=[inside] * 2,
        out_specs=inside,
        compiler_params=pltpu.CompilerParams(vmem_limit_bytes=16 * 2**20),
    )(mine, theirs)
    return out.reshape(-1)


def solution(mesh):
    placed = (P("ch", ("grp", "tm")), P(None, "grp"), P(), P(("grp", "tm"), "sub", None, None))
    return jax.shard_map(
        body, mesh=mesh, in_specs=placed, out_specs=P(("grp", "tm", "sub")), check_vma=False
    )
```
